32 devices in a mesh: ens: 2 (over x), col: 16 (over z, y, core).
Axes of the slice: x: 2, y: 2, z: 4, core: 2. Of those that a mesh axis runs over, the one named last changes fastest.
Arguments:
- gcm_state: float32 [4608, 128], P(('ens', 'col')), parts along dimension 0, may hold values from -6 to 6
- cloud_model_state: bfloat16 [9216, 32, 128], P(('ens', 'col')), parts along dimension 0, may hold values from -6 to 6
- owner: int32 [4608, 1], P(('ens', 'col')), parts along dimension 0, may hold values from 0 to 15; in each aligned block of 144 rows (0 to 143, 144 to 287, ...) at most 18 rows name the same one
- substeps: int32 [4608], P(('ens', 'col')), parts along dimension 0, may hold values from 1 to 2
- neighbours: int32 [512, 4], P(('ens', 'col')), parts along dimension 0, may hold values from 0 to 255, as said below
- mig_slot: int32 [4096], P(('ens', 'col')), parts along dimension 0, may hold values from 0 to 287, as said below
- mig_dest: int32 [4096, 1], P(('ens', 'col')), parts along dimension 0, may hold values from 0 to 15; in each aligned block of 128 rows (0 to 127, 128 to 255, ...) at most 16 rows name the same one
Outputs:
- gcm_new: float32 [4608, 128], P(('ens', 'col')), parts along dimension 0
- crm_new: bfloat16 [9216, 32, 128], P(('ens', 'col')), parts along dimension 0
- arrived: bfloat16 [8192, 32, 128], P(('ens', 'col')), parts along dimension 0
The draws below stay inside these ranges and needn't reach their ends.
There are 2 independent parts, one for each index of `ens`. The reference program is written for one: setup_inputs(seed, part) draws one part's arguments, and reference() takes and returns one part's arrays. A program takes and returns all parts, laid end to end along the dimension named above; each array names one. Nothing has to cross between parts.
Inputs may be any that keep to these rules, and one draw needn't show every extreme that they name: The 144 columns of one device name each owner at most 18 times. `mig_dest`: the 128 migrations of one device name each destination at most 16 times. `mig_slot`: the 128 slots listed by one device are distinct. neighbours 0 and 1 of element e lie 1 to 8 elements before e in Morton order and neighbours 2 and 3 1 to 8 after it, cyclically over 256; for every e that is a multiple of 16, neighbour 0 of e is exactly 8 before it and neighbour 3 of e + 15 exactly 8 after that one.
All inputs are finite; a program needn't handle non-finite values.
Results may differ from the reference program's by a relative error of at most 0.0033.
Values may be sent and summed in bfloat16 or wider, within the bound.
A program may use at most 128 MiB of HBM per device.

```python
import math
import jax
import jax.numpy as jnp
import numpy as np
from jax import lax

LEV = 64
CRMX = 32
SUBMAX = 2
ELEM_DEV = 16
MIG = 128
COLS_DEV = 144
REACH = 8
CAP = 18
SLOTS = 288
MCAP = 16
ARRIVE_DEV = 256
TOTAL = 2304
ELEMS = 256
ALL_SLOTS = 4608
MIG_ALL = 2048
ARRIVALS = 4096
N_COL = 16


def draw_neighbours(key, part):
    key = jax.random.fold_in(key, 11)
    distance = jax.random.randint(key, (ELEMS, 4), 1, REACH + 1)
    offsets = distance * jnp.array([-1, -1, 1, 1], jnp.int32)[None, :]
    element = jnp.arange(ELEMS, dtype=jnp.int32)
    inside = element % ELEM_DEV
    first_col = jnp.where(inside == 0, -REACH, offsets[:, 0])
    last_col = jnp.where(inside == ELEM_DEV - 1, REACH, offsets[:, 3])
    offsets = jnp.stack([first_col, offsets[:, 1], offsets[:, 2], last_col], axis=1)
    return jnp.mod(element[:, None] + offsets, ELEMS).astype(jnp.int32)


def draw_mig_slot(key, part):
    key = jax.random.fold_in(key, 23)
    device_count = MIG_ALL // MIG
    keys = jax.random.split(key, device_count)
    listed = jax.vmap(lambda single: jax.random.permutation(single, SLOTS)[:MIG])(keys)
    return listed.reshape(-1).astype(jnp.int32)


def with_ends(values, rng, smallest, high):
    longest = values.shape.index(max(values.shape))
    spots = []
    for shift in (0, 1):
        where = [jax.random.randint(jax.random.fold_in(rng, axis), (), 0, length) for axis, length in enumerate(values.shape)]
        where[longest] = (where[longest] + shift) % values.shape[longest]
        spots.append(tuple(where))
    return values.at[spots[0]].set(smallest).at[spots[1]].set(high)


def level_of(stream_key, shape, shards, least, top_value):
    factor_of, own = 1.0, jax.random.fold_in(stream_key, 6)
    for position, shards_of in shards:
        steps = jnp.exp(jax.random.uniform(jax.random.fold_in(own, position), (shards_of,), jnp.float32, least / len(shards), top_value / len(shards)))
        factor_of = factor_of * jnp.repeat(steps, shape[position] // shards_of).reshape([-1 if axis == position else 1 for axis in range(len(shape))])
    return factor_of


def assign_block(stream_key, own, number, rows, count, top, limit, skew):
    sequence = jax.random.permutation(stream_key, count)
    crowded, common = shares(count, rows * top, limit, skew, True), shares(count, rows * top, limit, skew, False)
    places = jnp.arange(count)

    def named(tallies, turn):
        used = int((tallies > 0).sum())
        fixed = max(1, used // 4)
        moved = fixed + (places - fixed + turn * (used - fixed)) % max(1, count - fixed)
        return jnp.zeros((count,), jnp.int32).at[sequence[jnp.where(places < fixed, places, moved)]].set(jnp.asarray(tallies, jnp.int32))

    tallies = jnp.where(number % 4 == 0, named(crowded, number // 4), named(common, number - number // 4 - 1))
    mixed = jax.random.permutation(jax.random.fold_in(own, 3), count)
    donor, sink = mixed[0:count // 2 * 2:2], mixed[1:count // 2 * 2:2]
    slack = jnp.minimum(tallies[donor] - 1, limit - tallies[sink]) // 2
    slack = jnp.where((donor == sequence[0]) | (sink == sequence[0]) | (tallies[sink] == 0), 0, jnp.maximum(slack, 0))
    moved = jax.random.randint(jax.random.fold_in(own, 4), (count // 2,), 0, 1 << 20) % (slack + 1)
    tallies = tallies.at[donor].add(-moved).at[sink].add(moved)
    items = jnp.searchsorted(jnp.cumsum(tallies), jnp.arange(rows * top), side="right").astype(jnp.int32)
    grid = items.reshape(top, rows).T
    grid = grid[jax.random.permutation(jax.random.fold_in(own, 1), rows)]
    turn = jax.random.randint(jax.random.fold_in(own, 2), (rows, 1), 0, top)
    return jnp.take_along_axis(grid, (jnp.arange(top)[None, :] + turn) % top, axis=1)


def shares(amount, total, most, skew, full):
    weights = [(1 << 20) // math.isqrt(grade ** skew) + 1 for grade in range(1, amount + 1)]
    largest = most if full else min(most, max(-(-total // amount), total * weights[0] // sum(weights)))
    least = 1 if total - largest >= amount - 1 else 0
    given, spare = [largest] + [least] * (amount - 1), total - largest - least * (amount - 1)
    while spare > 0:
        movable = [i for i in range(1, amount) if given[i] < largest] or [i for i in range(1, amount) if given[i] < most]
        pool, left = sum([weights[i] for i in movable]), spare
        for i in movable:
            addition = min(most - given[i], max(1, left * weights[i] // pool), spare)
            given[i] = given[i] + addition
            spare = spare - addition
    return np.array(given)


def normal_values(key, extent, spread, limit, cuts=(), kind=jnp.bfloat16):
    loudness = level_of(key, extent, cuts, -0.22, 0.18) if cuts else 1.0
    entries = jax.random.normal(key, extent, jnp.float32) * spread * loudness
    return jnp.minimum(jnp.maximum(entries, -limit), limit).astype(kind)


def setup_inputs(seed: int = 0, part: int = 0) -> dict:
    arg_keys = jax.random.split(jax.random.key(seed), 8)
    part_splits = jax.random.split(jax.random.fold_in(arg_keys[7], part), 8)
    gcm_state = normal_values(part_splits[0], (TOTAL, 2 * LEV), 1.0, 6.0, ((0, 16),), jnp.float32)
    cloud_model_state = normal_values(part_splits[1], (ALL_SLOTS, CRMX, 2 * LEV), 1.0, 6.0, ((0, 16),))
    owner_keys = jax.random.split(jax.random.fold_in(part_splits[2], 1), TOTAL // COLS_DEV)
    owner_turns = jax.random.permutation(jax.random.fold_in(part_splits[2], 3), TOTAL // COLS_DEV)
    owner = jax.vmap(lambda own, number: assign_block(jax.random.fold_in(part_splits[2], 2), own, number, COLS_DEV, N_COL, 1, CAP, 2))(owner_keys, owner_turns).reshape((TOTAL, 1))
    substeps = with_ends(jax.random.randint(part_splits[3], (TOTAL,), 1, SUBMAX + 1), jax.random.fold_in(part_splits[3], 1), 1, SUBMAX).astype(jnp.int32)
    neighbours = draw_neighbours(jax.random.fold_in(jax.random.fold_in(arg_keys[7], part), 71), part)
    mig_slot = draw_mig_slot(jax.random.fold_in(jax.random.fold_in(arg_keys[7], part), 71), part)
    mig_dest_keys = jax.random.split(jax.random.fold_in(part_splits[6], 1), MIG_ALL // MIG)
    mig_dest_turns = jax.random.permutation(jax.random.fold_in(part_splits[6], 3), MIG_ALL // MIG)
    mig_dest = jax.vmap(lambda own, number: assign_block(jax.random.fold_in(part_splits[6], 2), own, number, MIG, N_COL, 1, MCAP, 2))(mig_dest_keys, mig_dest_turns).reshape((MIG_ALL, 1))
    return dict(gcm_state=gcm_state, cloud_model_state=cloud_model_state, owner=owner, substeps=substeps, neighbours=neighbours, mig_slot=mig_slot, mig_dest=mig_dest)


EDGE_RATE = 0.2
ACROSS_RATE = 0.2
VERTICAL_RATE = 0.15
NUDGE_RATE = 0.3
PHASE_RATE = 0.25


def ranks(targets, groups, model_width):
    per_group = targets.shape[0] // groups
    table = targets.reshape(groups, per_group)
    hits = (table[:, :, None] == jnp.arange(model_width, dtype=jnp.int32)[None, None, :]).astype(jnp.int32)
    before = jnp.cumsum(hits, axis=1) - hits
    return jnp.sum(before * hits, axis=2).reshape(-1).astype(jnp.int32)


def crm_steps(column_state, forcing, counts):
    slot_number, across_flux, model_width = column_state.shape
    level_count = model_width // 2
    state_field = column_state.astype(jnp.float32)
    anchor = jnp.mean(state_field, axis=1)
    signs = jnp.array([1.0, -1.0], jnp.float32)[None, None, :, None]
    for step in range(SUBMAX):
        beside = jnp.roll(state_field, 1, axis=1) + jnp.roll(state_field, -1, axis=1) - 2.0 * state_field
        split_point = state_field.reshape(slot_number, across_flux, 2, level_count)
        padded = jnp.pad(split_point, ((0, 0), (0, 0), (0, 0), (1, 1)), mode="edge")
        vertical_flux = (padded[..., 2:] + padded[..., :-2] - 2.0 * split_point).reshape(slot_number, across_flux, model_width)
        phase = PHASE_RATE * jnp.tanh(split_point[:, :, 1, :] - 0.5 * split_point[:, :, 0, :])
        phases = (phase[:, :, None, :] * signs).reshape(slot_number, across_flux, model_width)
        average = jnp.mean(state_field, axis=1, keepdims=True)
        moved = state_field + ACROSS_RATE * beside + VERTICAL_RATE * vertical_flux + NUDGE_RATE * (forcing[:, None, :] - average) + phases
        active = (step < counts)[:, None, None]
        state_field = jnp.where(active, moved, state_field)
    divisor = jnp.maximum(counts, 1).astype(state_field.dtype)[:, None]
    tendency = (jnp.mean(state_field, axis=1) - anchor) / divisor
    return state_field.astype(jnp.bfloat16), tendency


def reference(gcm_state, cloud_model_state, owner, substeps, neighbours, mig_slot, mig_dest):
    model_width = gcm_state.shape[1]
    means = jnp.mean(gcm_state.reshape(ELEMS, 9, model_width), axis=1)
    beside_all = jnp.sum(means[neighbours], axis=1)
    dynamic_state = gcm_state + jnp.repeat(EDGE_RATE * (beside_all - 4.0 * means), 9, axis=0)
    target = owner[:, 0]
    source = jnp.arange(TOTAL, dtype=jnp.int32) // COLS_DEV
    slot = target * SLOTS + source * CAP + ranks(target, N_COL, N_COL)
    forcing = jnp.zeros((ALL_SLOTS, model_width), gcm_state.dtype).at[slot].set(dynamic_state)
    counts = jnp.zeros((ALL_SLOTS,), jnp.int32).at[slot].set(substeps)

    def per_owner(block):
        return crm_steps(block[0], block[1], block[2])

    after, tendency = lax.map(per_owner, (cloud_model_state.reshape(N_COL, SLOTS, CRMX, model_width), forcing.reshape(N_COL, SLOTS, model_width), counts.reshape(N_COL, SLOTS)))
    after = after.reshape(ALL_SLOTS, CRMX, model_width)
    gcm_new = dynamic_state + tendency.reshape(ALL_SLOTS, model_width)[slot]
    mover = jnp.arange(MIG_ALL, dtype=jnp.int32) // MIG
    from_slot = mover * SLOTS + mig_slot
    move_dest = mig_dest[:, 0]
    into = move_dest * ARRIVE_DEV + mover * MCAP + ranks(move_dest, N_COL, N_COL)
    arrived = jnp.zeros((ARRIVALS, CRMX, model_width), jnp.bfloat16).at[into].set(after[from_slot])
    crm_new = after.at[from_slot].set(jnp.zeros((CRMX, model_width), jnp.bfloat16))
    return gcm_new, crm_new, arrived
```

```python
import functools

import jax
import jax.numpy as jnp
from jax import lax
from jax.experimental import pallas as pl
from jax.experimental.pallas import tpu as pltpu
from jax.sharding import PartitionSpec as P

F32, BF16, I32 = jnp.float32, jnp.bfloat16, jnp.int32
MESH = pl.DeviceIdType.MESH
GROUP = 8


def iota(shape, dim):
    return lax.broadcasted_iota(I32, shape, dim)


def ones_where(condition, dtype=BF16):
    return jnp.where(condition, 1.0, 0.0).astype(dtype)


def exact(a, b):
    return jnp.dot(a, b, preferred_element_type=F32, precision=lax.Precision.HIGHEST)


def fast(a, b):
    return jnp.dot(a, b, preferred_element_type=F32)


def step_matrices(across, width):
    size = GROUP * across
    shift = across.bit_length() - 1
    row, col = iota((size, size), 0), iota((size, size), 1)
    same = (row >> shift) == (col >> shift)
    gap = (row - col) & (across - 1)
    beside = jnp.where((gap == 1) | (gap == across - 1), 1.0, 0.0)
    middle = jnp.where(gap == 0, 3.0, 0.0)
    left = jnp.where(same, beside + middle - 1.5 / across, 0.0).astype(BF16)
    half = width // 2
    source, level = iota((width, 2 * width), 0), iota((width, 2 * width), 1)
    inside = (source < half) == (level < half)
    near = jnp.where(jnp.abs(source - level) == 1, 0.75, 0.0)
    edge = (level == 0) | (level == half - 1) | (level == half) | (level == width - 1)
    near = near - jnp.where(source == level, jnp.where(edge, 0.75, 1.5), 0.0)
    vertical = jnp.where(inside, near, 0.0)
    target = level - width
    sign = jnp.where(target < half, 1.0, -1.0)
    of_level = (source & (half - 1)) == (target & (half - 1))
    phase = jnp.where(of_level, jnp.where(source < half, -0.5, 1.0) * sign, 0.0)
    right = jnp.where(level < width, vertical, phase).astype(BF16)
    rows = iota((GROUP, size), 0)
    total = ones_where(rows == (iota((GROUP, size), 1) >> shift))
    return left, right, total


def one_step(state, forcing, left, right, across, width):
    linear = fast(left, state)
    levels = fast(state, right)
    pushed = jnp.broadcast_to((1.5 * forcing)[:, None, :], (GROUP, across, width))
    pushed = pushed.reshape(GROUP * across, width)
    return 0.2 * (linear + levels[:, :width] + pushed) + 0.25 * jnp.tanh(levels[:, width:])


def kernel(n, cap, capp, mcap,
           gcm_ref, cloud_ref, owner_col_ref, owner_row_ref, substeps_ref, neigh_ref,
           mig_row_ref, pick_ref,
           new_ref, crm_ref, arrived_ref,
           ext, dyn, fsend, frecv, fc, keep, tend, tsend, trecv, after, depart,
           halo_send, halo_recv, f_send, f_recv, t_send, t_recv, m_send, m_recv, own_sem):
    me = lax.axis_index("col")
    cols, width = gcm_ref.shape
    slots, across, _ = cloud_ref.shape
    elements = cols // 9
    margin = elements // 2
    table = n * capp
    shift = capp.bit_length() - 1
    right_dev, left_dev = lax.rem(me + 1, n), lax.rem(me + n - 1, n)

    barrier = pltpu.get_barrier_semaphore()

    def greet(k, carry):
        pl.semaphore_signal(barrier, inc=1, device_id={"col": lax.rem(me + k, n)}, device_id_type=MESH)
        return carry

    lax.fori_loop(1, n, greet, 0)

    gcm = gcm_ref[...]
    place = iota((elements, cols), 1) - 9 * iota((elements, cols), 0)
    member = ones_where((place >= 0) & (place < 9), F32)
    means = exact(member, gcm) * (1.0 / 9.0)
    ext[pl.ds(margin, elements), :] = means
    pl.semaphore_wait(barrier, n - 1)

    up = pltpu.make_async_remote_copy(
        src_ref=ext.at[pl.ds(elements, margin)], dst_ref=ext.at[pl.ds(0, margin)],
        send_sem=halo_send.at[0], recv_sem=halo_recv.at[0],
        device_id={"col": right_dev}, device_id_type=MESH)
    down = pltpu.make_async_remote_copy(
        src_ref=ext.at[pl.ds(margin, margin)], dst_ref=ext.at[pl.ds(margin + elements, margin)],
        send_sem=halo_send.at[1], recv_sem=halo_recv.at[1],
        device_id={"col": left_dev}, device_id_type=MESH)
    up.start()
    down.start()

    owner_row = owner_row_ref[...]
    hits = iota((n, cols), 0) == owner_row
    earlier = ones_where(iota((cols, cols), 0) < iota((cols, cols), 1))
    before = fast(ones_where(hits), earlier)
    rank = jnp.sum(jnp.where(hits, before, 0.0), axis=0, keepdims=True).astype(I32)
    place_row = owner_row * capp + rank
    scatter = ones_where(iota((table, cols), 0) == place_row)
    gone = iota((slots, mig_row_ref.shape[1]), 0) == mig_row_ref[...]
    gone = jnp.max(jnp.where(gone, 1.0, 0.0), axis=1, keepdims=True)
    keep[...] = jnp.broadcast_to(1.0 - gone, (slots, width))
    after[pl.ds(slots, 1)] = jnp.zeros((1, across, width), BF16)

    ids = neigh_ref[...] - me * elements + margin
    span = elements * n
    ids = jnp.where(ids < 0, ids + span, ids)
    ids = jnp.where(ids >= span, ids - span, ids)
    wide = iota((elements, elements + 2 * margin), 1)
    weights = jnp.where(wide == iota((elements, elements + 2 * margin), 0) + margin, -4.0, 0.0)
    for k in range(neigh_ref.shape[1]):
        weights = weights + jnp.where(wide == ids[:, k:k + 1], 1.0, 0.0)
    spread_gap = iota((cols, elements), 0) - 9 * iota((cols, elements), 1)
    spread = ones_where((spread_gap >= 0) & (spread_gap < 9), F32)

    up.wait()
    down.wait()
    change = 0.2 * exact(weights, ext[...])
    state = gcm + exact(spread, change)
    dyn[...] = state

    payload = jnp.concatenate(
        [state.astype(BF16), jnp.broadcast_to(substeps_ref[...].astype(F32), (cols, width)).astype(BF16)],
        axis=1)
    fsend[...] = fast(scatter, payload).astype(BF16).reshape(n, capp, 2 * width)

    def forcing_copy(k):
        return pltpu.make_async_remote_copy(
            src_ref=fsend.at[lax.rem(me + k, n)], dst_ref=frecv.at[me],
            send_sem=f_send.at[k], recv_sem=f_recv.at[k],
            device_id={"col": lax.rem(me + k, n)}, device_id_type=MESH)

    def start(copy):
        def body(k, carry):
            copy(k).start()
            return carry
        lax.fori_loop(1, n, body, 0)

    def wait_recv(copy):
        def body(k, carry):
            copy(k).wait_recv()
            return carry
        lax.fori_loop(1, n, body, 0)

    def wait_send(copy):
        def body(k, carry):
            copy(k).wait_send()
            return carry
        lax.fori_loop(1, n, body, 0)

    start(forcing_copy)
    frecv[me] = fsend[me]

    left, right, total = step_matrices(across, width)
    p_lane = iota((slots, table), 1)
    q_lane = (p_lane >> shift) * cap + (p_lane & (capp - 1))
    compact = ones_where((q_lane == iota((slots, table), 0)) & ((p_lane & (capp - 1)) < cap))

    wait_recv(forcing_copy)
    fc[...] = fast(compact, frecv[...].reshape(table, 2 * width))

    def chunk(c, carry):
        at = pl.multiple_of(c * GROUP, GROUP)
        rows = pl.ds(at, GROUP)
        forcing = fc[rows, 0:width]
        count = fc[rows, width:2 * width]
        begin = cloud_ref[rows].reshape(GROUP * across, width)
        lanes = jnp.broadcast_to(count[:, None, :], (GROUP, across, width))
        lanes = lanes.reshape(GROUP * across, width)
        first = one_step(begin, forcing, left, right, across, width)
        first = jnp.where(lanes > 0.5, first, begin.astype(F32)).astype(BF16)
        second = one_step(first, forcing, left, right, across, width)
        second = jnp.where(lanes > 1.5, second, first.astype(F32))
        final = second.astype(BF16)
        gain = fast(total, final) - fast(total, begin)
        tend[rows, :] = gain * (1.0 / across) / jnp.maximum(count, 1.0)
        after[rows] = final.reshape(GROUP, across, width)
        stay = jnp.broadcast_to(keep[rows, :][:, None, :], (GROUP, across, width))
        crm_ref[rows] = (second.reshape(GROUP, across, width) * stay).astype(BF16)
        return carry

    lax.fori_loop(0, slots // GROUP, chunk, 0)

    p_row = iota((table, slots), 0)
    q_row = (p_row >> shift) * cap + (p_row & (capp - 1))
    expand = ones_where((q_row == iota((table, slots), 1)) & ((p_row & (capp - 1)) < cap))
    tsend[...] = fast(expand, tend[...].astype(BF16)).astype(BF16).reshape(n, capp, width)

    def tendency_copy(k):
        return pltpu.make_async_remote_copy(
            src_ref=tsend.at[lax.rem(me + k, n)], dst_ref=trecv.at[me],
            send_sem=t_send.at[k], recv_sem=t_recv.at[k],
            device_id={"col": lax.rem(me + k, n)}, device_id_type=MESH)

    start(tendency_copy)
    trecv[me] = tsend[me]

    def pack(dest):
        base = dest * mcap
        for r in range(mcap):
            depart[base + r] = after[pick_ref[base + r]]

    def mig_copy(k):
        dest = lax.rem(me + k, n)
        return pltpu.make_async_remote_copy(
            src_ref=depart.at[pl.ds(dest * mcap, mcap)],
            dst_ref=arrived_ref.at[pl.ds(me * mcap, mcap)],
            send_sem=m_send.at[k], recv_sem=m_recv.at[k],
            device_id={"col": dest}, device_id_type=MESH)

    def depart_body(k, carry):
        pack(lax.rem(me + k, n))
        mig_copy(k).start()
        return carry

    lax.fori_loop(1, n, depart_body, 0)
    pack(me)
    own = pltpu.make_async_copy(
        depart.at[pl.ds(me * mcap, mcap)], arrived_ref.at[pl.ds(me * mcap, mcap)], own_sem)
    own.start()

    owner_col = owner_col_ref[...]
    hits_col = iota((cols, n), 1) == owner_col
    earlier_col = ones_where(iota((cols, cols), 1) < iota((cols, cols), 0))
    before_col = fast(earlier_col, ones_where(hits_col))
    rank_col = jnp.sum(jnp.where(hits_col, before_col, 0.0), axis=1, keepdims=True).astype(I32)
    place_col = owner_col * capp + rank_col
    gather = ones_where(iota((cols, table), 1) == place_col)
    wait_recv(tendency_copy)
    new_ref[...] = dyn[...] + fast(gather, trecv[...].reshape(table, width))

    wait_recv(mig_copy)
    wait_send(forcing_copy)
    wait_send(tendency_copy)
    wait_send(mig_copy)
    own.wait()


def per_device(gcm_state, cloud_model_state, owner, substeps, neighbours, mig_slot, mig_dest):
    n = lax.axis_size("col")
    cols, width = gcm_state.shape
    slots, across, _ = cloud_model_state.shape
    cap = slots // n
    capp = 16
    while capp < cap:
        capp *= 2
    listed = mig_slot.shape[0]
    mcap = max(2, 2 * listed // n)
    elements = cols // 9
    dest = mig_dest[:, 0]
    order = jnp.arange(listed, dtype=I32)
    rank = jnp.sum(((dest[:, None] == dest[None, :]) & (order[None, :] < order[:, None])).astype(I32), axis=1)
    place = dest * mcap + rank
    spots = jnp.arange(n * mcap, dtype=I32)
    pick = jnp.min(jnp.where(place[None, :] == spots[:, None], mig_slot[None, :], slots), axis=1)
    vmem = pl.BlockSpec(memory_space=pltpu.VMEM)
    dma = pltpu.SemaphoreType.DMA
    table = n * capp
    return pl.pallas_call(
        functools.partial(kernel, n, cap, capp, mcap),
        out_shape=(
            jax.ShapeDtypeStruct((cols, width), F32),
            jax.ShapeDtypeStruct((slots, across, width), BF16),
            jax.ShapeDtypeStruct((n * mcap, across, width), BF16),
        ),
        in_specs=[vmem] * 7 + [pl.BlockSpec(memory_space=pltpu.SMEM)],
        out_specs=(vmem, vmem, pl.BlockSpec(memory_space=pl.ANY)),
        scratch_shapes=[
            pltpu.VMEM((2 * elements, width), F32),
            pltpu.VMEM((cols, width), F32),
            pltpu.VMEM((n, capp, 2 * width), BF16),
            pltpu.VMEM((n, capp, 2 * width), BF16),
            pltpu.VMEM((slots, 2 * width), F32),
            pltpu.VMEM((slots, width), F32),
            pltpu.VMEM((slots, width), F32),
            pltpu.VMEM((n, capp, width), BF16),
            pltpu.VMEM((n, capp, width), BF16),
            pltpu.VMEM((slots + 1, across, width), BF16),
            pltpu.VMEM((n * mcap, across, width), BF16),
            dma((2,)), dma((2,)), dma((n,)), dma((n,)), dma((n,)), dma((n,)), dma((n,)), dma((n,)),
            dma,
        ],
        compiler_params=pltpu.CompilerParams(
            collective_id=0, has_side_effects=True, vmem_limit_bytes=40 * 1024 * 1024),
        cost_estimate=pl.CostEstimate(flops=5 * 10**9, bytes_accessed=10**7, transcendentals=2 * 10**6),
    )(
        gcm_state, cloud_model_state, owner, owner.reshape(1, cols), substeps.reshape(cols, 1),
        neighbours, mig_slot.reshape(1, listed), pick,
    )


def solution(mesh):
    wide, deep, flat = P(("ens", "col"), None), P(("ens", "col"), None, None), P(("ens", "col"))
    return jax.shard_map(
        per_device, mesh=mesh,
        in_specs=(wide, deep, wide, flat, wide, flat, wide),
        out_specs=(wide, deep, deep), check_vma=False,
    )
```

```python
import functools

import jax
import jax.numpy as jnp
from jax import lax
from jax.experimental import pallas as pl
from jax.experimental.pallas import tpu as pltpu
from jax.sharding import PartitionSpec as P

F32, BF16, I32 = jnp.float32, jnp.bfloat16, jnp.int32
MESH = pl.DeviceIdType.MESH
GROUP = 8
TOGETHER = 4
BATCH = 16
EARLY = 4


def iota(shape, dim):
    return lax.broadcasted_iota(I32, shape, dim)


def ones_where(condition, dtype=BF16):
    return jnp.where(condition, 1.0, 0.0).astype(dtype)


def exact(a, b):
    return jnp.dot(a, b, preferred_element_type=F32, precision=lax.Precision.HIGHEST)


def fast(a, b):
    return jnp.dot(a, b, preferred_element_type=F32)


def step_matrices(across, width):
    size = GROUP * across
    shift = across.bit_length() - 1
    row, col = iota((size, size), 0), iota((size, size), 1)
    same = (row >> shift) == (col >> shift)
    gap = (row - col) & (across - 1)
    beside = jnp.where((gap == 1) | (gap == across - 1), 1.0, 0.0)
    middle = jnp.where(gap == 0, 3.0, 0.0)
    left = jnp.where(same, beside + middle - 1.5 / across, 0.0).astype(BF16)
    half = width // 2
    source, level = iota((width, 2 * width), 0), iota((width, 2 * width), 1)
    inside = (source < half) == (level < half)
    near = jnp.where(jnp.abs(source - level) == 1, 0.75, 0.0)
    edge = (level == 0) | (level == half - 1) | (level == half) | (level == width - 1)
    near = near - jnp.where(source == level, jnp.where(edge, 0.75, 1.5), 0.0)
    vertical = jnp.where(inside, near, 0.0)
    target = level - width
    sign = jnp.where(target < half, 1.0, -1.0)
    of_level = (source & (half - 1)) == (target & (half - 1))
    phase = jnp.where(of_level, jnp.where(source < half, -0.5, 1.0) * sign, 0.0)
    right = jnp.where(level < width, vertical, phase).astype(BF16)
    rows = iota((GROUP, size), 0)
    total = ones_where(rows == (iota((GROUP, size), 1) >> shift))
    return left, right, total


def steps(states, forcings, counts, left, right, across, width):
    size = GROUP * across
    spread = lambda rows: jnp.broadcast_to(rows[:, None, :], (GROUP, across, width)).reshape(size, width)
    states = list(states)
    for least in (0.5, 1.5):
        linear = [fast(left, state) for state in states]
        levels = [fast(state, right) for state in states]
        moved = [
            0.2 * (a + b[:, :width] + spread(1.5 * f)) + 0.25 * jnp.tanh(b[:, width:])
            for a, b, f in zip(linear, levels, forcings)
        ]
        states = [
            jnp.where(spread(count) > least, new, old.astype(F32)).astype(BF16)
            for new, old, count in zip(moved, states, counts)
        ]
    return states


def kernel(n, cap, capp, mcap,
           gcm_hbm, cloud_hbm, owner_ref, substeps_ref, neigh_ref, slot_ref, dest_ref,
           new_ref, crm_ref, arrived_ref,
           gcm_ref, ext, dyn, fsend, frecv, fc, fbatch, keep, tend, tsend, trecv, work, depart,
           pick_v, pick,
           halo_send, halo_recv, f_send, f_recv, t_send, t_recv, m_send, m_recv, own_sem,
           gcm_sem, cloud_sem, pick_sem):
    me = lax.axis_index("col")
    cols, width = gcm_hbm.shape
    slots, across, _ = cloud_hbm.shape
    listed = slot_ref.shape[1]
    elements = cols // 9
    margin = elements // 2
    table = n * capp
    spots = n * mcap
    shift = capp.bit_length() - 1
    right_dev, left_dev = lax.rem(me + 1, n), lax.rem(me + n - 1, n)

    gcm_copy = pltpu.make_async_copy(gcm_hbm, gcm_ref, gcm_sem)
    gcm_copy.start()
    cloud_copy = pltpu.make_async_copy(cloud_hbm, work.at[pl.ds(0, slots)], cloud_sem)
    cloud_copy.start()
    barrier = pltpu.get_barrier_semaphore()

    def greet(k, carry):
        pl.semaphore_signal(barrier, inc=1, device_id={"col": lax.rem(me + k, n)}, device_id_type=MESH)
        return carry

    lax.fori_loop(1, n, greet, 0)

    gcm_copy.wait()
    gcm = gcm_ref[...]
    place = iota((elements, cols), 1) - 9 * iota((elements, cols), 0)
    member = ones_where((place >= 0) & (place < 9), F32)
    means = exact(member, gcm) * (1.0 / 9.0)
    ext[pl.ds(margin, elements), :] = means
    pl.semaphore_wait(barrier, n - 1)

    up = pltpu.make_async_remote_copy(
        src_ref=ext.at[pl.ds(elements, margin)], dst_ref=ext.at[pl.ds(0, margin)],
        send_sem=halo_send.at[0], recv_sem=halo_recv.at[0],
        device_id={"col": right_dev}, device_id_type=MESH)
    down = pltpu.make_async_remote_copy(
        src_ref=ext.at[pl.ds(margin, margin)], dst_ref=ext.at[pl.ds(margin + elements, margin)],
        send_sem=halo_send.at[1], recv_sem=halo_recv.at[1],
        device_id={"col": left_dev}, device_id_type=MESH)
    up.start()
    down.start()

    owner_row = owner_ref[...]
    hits = iota((n, cols), 0) == owner_row
    earlier = ones_where(iota((cols, cols), 0) < iota((cols, cols), 1))
    before = fast(ones_where(hits), earlier)
    rank = jnp.sum(jnp.where(hits, before, 0.0), axis=0, keepdims=True).astype(I32)
    place_row = owner_row * capp + rank
    scatter = ones_where(iota((table, cols), 0) == place_row)
    substeps = jnp.broadcast_to(substeps_ref[...].astype(F32), (width, cols)).astype(BF16)
    sent_counts = lax.dot_general(scatter, substeps, (((1,), (1,)), ((), ())), preferred_element_type=F32)
    fsend[:, :, width:2 * width] = sent_counts.astype(BF16).reshape(n, capp, width)

    ids = neigh_ref[...] - me * elements + margin
    span = elements * n
    ids = jnp.where(ids < 0, ids + span, ids)
    ids = jnp.where(ids >= span, ids - span, ids)
    tall = iota((elements + 2 * margin, elements), 0)
    weights = jnp.where(tall == iota((elements + 2 * margin, elements), 1) + margin, -4.0, 0.0)
    for k in range(neigh_ref.shape[0]):
        weights = weights + jnp.where(tall == ids[k:k + 1, :], 1.0, 0.0)
    spread_gap = iota((cols, elements), 0) - 9 * iota((cols, elements), 1)
    spread = ones_where((spread_gap >= 0) & (spread_gap < 9), F32)
    per_column = fast(spread.astype(BF16), weights.T.astype(BF16))

    up.wait()
    down.wait()
    state = gcm + 0.2 * exact(per_column, ext[...])
    dyn[...] = state
    fsend[:, :, 0:width] = fast(scatter, state.astype(BF16)).astype(BF16).reshape(n, capp, width)

    def forcing_copy(k):
        return pltpu.make_async_remote_copy(
            src_ref=fsend.at[lax.rem(me + k, n)], dst_ref=frecv.at[me],
            send_sem=f_send.at[k], recv_sem=f_recv.at[k],
            device_id={"col": lax.rem(me + k, n)}, device_id_type=MESH)

    def start(copy):
        def body(k, carry):
            copy(k).start()
            return carry
        lax.fori_loop(1, n, body, 0)

    def wait_recv(copy):
        def body(k, carry):
            copy(k).wait_recv()
            return carry
        lax.fori_loop(1, n, body, 0)

    def wait_send(copy):
        def body(k, carry):
            copy(k).wait_send()
            return carry
        lax.fori_loop(1, n, body, 0)

    start(forcing_copy)
    frecv[me] = fsend[me]

    slot_row, dest_row = slot_ref[...], dest_ref[...]
    slot_col = jnp.broadcast_to(slot_row, (listed, listed)).T
    dest_col = jnp.broadcast_to(dest_row, (listed, listed)).T
    same = (dest_col == dest_row) & (iota((listed, listed), 1) < iota((listed, listed), 0))
    place_mig = dest_col[:, 0:1] * mcap + jnp.sum(jnp.where(same, 1, 0), axis=1, keepdims=True)
    found = iota((listed, spots), 1) == place_mig
    chosen = jnp.sum(jnp.where(found, slot_col[:, 0:1] - slots, 0), axis=0, keepdims=True) + slots
    pick_v[...] = chosen
    pick_copy = pltpu.make_async_copy(pick_v, pick, pick_sem)
    pick_copy.start()
    gone = iota((slots, listed), 0) == slot_row
    gone = jnp.max(jnp.where(gone, 1.0, 0.0), axis=1, keepdims=True)
    keep[...] = jnp.broadcast_to(1.0 - gone, (slots, width))
    work[pl.ds(slots, 1)] = jnp.zeros((1, across, width), BF16)
    fc[pl.ds(slots, 8), :] = jnp.zeros((8, 2 * width), F32)
    left, right, total = step_matrices(across, width)
    p_lane = iota((slots, table), 1)
    q_lane = (p_lane >> shift) * cap + (p_lane & (capp - 1))
    compact = ones_where((q_lane == iota((slots, table), 0)) & ((p_lane & (capp - 1)) < cap))
    pick_copy.wait()
    cloud_copy.wait()

    wait_recv(forcing_copy)
    fc[pl.ds(0, slots), :] = fast(compact, frecv[...].reshape(table, 2 * width))

    def partner(j):
        half = lax.div(j + 1, 2)
        return n // 2 + jnp.where(lax.rem(j, 2) == 1, -half, half)

    def mig_copy(j):
        k = partner(j)
        return pltpu.make_async_remote_copy(
            src_ref=depart.at[pl.ds(j * mcap, mcap)],
            dst_ref=arrived_ref.at[pl.ds(me * mcap, mcap)],
            send_sem=m_send.at[k], recv_sem=m_recv.at[k],
            device_id={"col": lax.rem(me + k, n)}, device_id_type=MESH)

    per_batch = max(1, BATCH // mcap)
    early = EARLY * per_batch
    size = GROUP * across

    def early_body(b, carry):
        for i in range(BATCH):
            j = b * per_batch + i // mcap
            at = pick[0, lax.rem(me + partner(j), n) * mcap + i % mcap]
            depart[b * BATCH + i] = work[at]
            fbatch[i:i + 1, :] = fc[pl.ds(at, 1), :]
        forcings, counts, states = [], [], []
        for g in range(BATCH // GROUP):
            states.append(depart[pl.ds(b * BATCH + g * GROUP, GROUP)].reshape(size, width))
            forcings.append(fbatch[g * GROUP:(g + 1) * GROUP, 0:width])
            counts.append(fbatch[g * GROUP:(g + 1) * GROUP, width:2 * width])
        finals = steps(states, forcings, counts, left, right, across, width)
        for g, final in enumerate(finals):
            depart[pl.ds(b * BATCH + g * GROUP, GROUP)] = final.reshape(GROUP, across, width)
        for j in range(per_batch):
            mig_copy(b * per_batch + j).start()
        return carry

    lax.fori_loop(0, EARLY, early_body, 0)

    def chunk(c, carry):
        rows = [pl.ds(pl.multiple_of((c * TOGETHER + g) * GROUP, GROUP), GROUP) for g in range(TOGETHER)]
        forcings = [fc[row, 0:width] for row in rows]
        counts = [fc[row, width:2 * width] for row in rows]
        stays = [keep[row, :] for row in rows]
        begins = [work[row].reshape(size, width) for row in rows]
        finals = steps(begins, forcings, counts, left, right, across, width)
        gains = [fast(total, final) - fast(total, begin) for final, begin in zip(finals, begins)]
        for row, final, gain, count, stay in zip(rows, finals, gains, counts, stays):
            tend[row, :] = gain * (1.0 / across) / jnp.maximum(count, 1.0)
            work[row] = final.reshape(GROUP, across, width)
            stay = jnp.broadcast_to(stay[:, None, :], (GROUP, across, width)).astype(BF16)
            crm_ref[row] = final.reshape(GROUP, across, width) * stay
        return carry

    lax.fori_loop(0, slots // (GROUP * TOGETHER), chunk, 0)

    p_row = iota((table, slots), 0)
    q_row = (p_row >> shift) * cap + (p_row & (capp - 1))
    expand = ones_where((q_row == iota((table, slots), 1)) & ((p_row & (capp - 1)) < cap))
    tsend[...] = fast(expand, tend[...].astype(BF16)).astype(BF16).reshape(n, capp, width)

    def tendency_copy(k):
        return pltpu.make_async_remote_copy(
            src_ref=tsend.at[lax.rem(me + k, n)], dst_ref=trecv.at[me],
            send_sem=t_send.at[k], recv_sem=t_recv.at[k],
            device_id={"col": lax.rem(me + k, n)}, device_id_type=MESH)

    start(tendency_copy)
    trecv[me] = tsend[me]

    def pack(j, dest):
        for r in range(mcap):
            depart[j * mcap + r] = work[pick[0, dest * mcap + r]]

    def depart_body(j, carry):
        pack(j, lax.rem(me + partner(j), n))
        mig_copy(j).start()
        return carry

    lax.fori_loop(early, n - 1, depart_body, 0)
    pack(n - 1, me)
    own = pltpu.make_async_copy(
        depart.at[pl.ds((n - 1) * mcap, mcap)], arrived_ref.at[pl.ds(me * mcap, mcap)], own_sem)
    own.start()

    wait_recv(tendency_copy)
    back = lax.dot_general(
        scatter, trecv[...].reshape(table, width), (((0,), (0,)), ((), ())), preferred_element_type=F32)
    new_ref[...] = dyn[...] + back

    wait_send(forcing_copy)
    wait_send(tendency_copy)

    def finish(j, carry):
        mig_copy(j).wait()
        return carry

    lax.fori_loop(0, n - 1, finish, 0)
    own.wait()


def per_device(gcm_state, cloud_model_state, owner, substeps, neighbours, mig_slot, mig_dest):
    n = lax.axis_size("col")
    cols, width = gcm_state.shape
    slots, across, _ = cloud_model_state.shape
    cap = slots // n
    capp = 16
    while capp < cap:
        capp *= 2
    listed = mig_slot.shape[0]
    mcap = max(2, 2 * listed // n)
    elements = cols // 9
    vmem = pl.BlockSpec(memory_space=pltpu.VMEM)
    dma = pltpu.SemaphoreType.DMA
    table = n * capp
    return pl.pallas_call(
        functools.partial(kernel, n, cap, capp, mcap),
        out_shape=(
            jax.ShapeDtypeStruct((cols, width), F32),
            jax.ShapeDtypeStruct((slots, across, width), BF16),
            jax.ShapeDtypeStruct((n * mcap, across, width), BF16),
        ),
        in_specs=[pl.BlockSpec(memory_space=pltpu.HBM)] * 2 + [vmem] * 5,
        out_specs=(vmem, vmem, pl.BlockSpec(memory_space=pltpu.HBM)),
        scratch_shapes=[
            pltpu.VMEM((cols, width), F32),
            pltpu.VMEM((2 * elements, width), F32),
            pltpu.VMEM((cols, width), F32),
            pltpu.VMEM((n, capp, 2 * width), BF16),
            pltpu.VMEM((n, capp, 2 * width), BF16),
            pltpu.VMEM((slots + 8, 2 * width), F32),
            pltpu.VMEM((BATCH, 2 * width), F32),
            pltpu.VMEM((slots, width), F32),
            pltpu.VMEM((slots, width), F32),
            pltpu.VMEM((n, capp, width), BF16),
            pltpu.VMEM((n, capp, width), BF16),
            pltpu.VMEM((slots + 1, across, width), BF16),
            pltpu.VMEM((n * mcap, across, width), BF16),
            pltpu.VMEM((1, n * mcap), I32),
            pltpu.SMEM((1, n * mcap), I32),
            dma((2,)), dma((2,)), dma((n,)), dma((n,)), dma((n,)), dma((n,)), dma((n,)), dma((n,)),
            dma, dma, dma, dma,
        ],
        compiler_params=pltpu.CompilerParams(
            collective_id=0, has_side_effects=True, vmem_limit_bytes=40 * 1024 * 1024),
        cost_estimate=pl.CostEstimate(flops=5 * 10**9, bytes_accessed=10**7, transcendentals=2 * 10**6),
    )(
        gcm_state, cloud_model_state, owner.reshape(1, cols), substeps.reshape(1, cols),
        neighbours.T, mig_slot.reshape(1, listed), mig_dest.reshape(1, listed),
    )


def solution(mesh):
    wide, deep, flat = P(("ens", "col"), None), P(("ens", "col"), None, None), P(("ens", "col"))
    return jax.shard_map(
        per_device, mesh=mesh,
        in_specs=(wide, deep, wide, flat, wide, flat, wide),
        out_specs=(wide, deep, deep), check_vma=False,
    )
```

```python
import functools

import jax
import jax.numpy as jnp
from jax import lax
from jax.experimental import pallas as pl
from jax.experimental.pallas import tpu as pltpu
from jax.sharding import PartitionSpec as P

F32, BF16, I32 = jnp.float32, jnp.bfloat16, jnp.int32
MESH = pl.DeviceIdType.MESH
GROUP = 8
TOGETHER = 4
BATCH = 16
EARLY = 3
PIECES = 2
RAW = 2


def iota(shape, dim):
    return lax.broadcasted_iota(I32, shape, dim)


def ones_where(condition, dtype=BF16):
    return jnp.where(condition, 1.0, 0.0).astype(dtype)


def exact(a, b):
    return jnp.dot(a, b, preferred_element_type=F32, precision=lax.Precision.HIGHEST)


def fast(a, b):
    return jnp.dot(a, b, preferred_element_type=F32)


def step_matrices(across, width):
    size = GROUP * across
    shift = across.bit_length() - 1
    row, col = iota((size, size), 0), iota((size, size), 1)
    same = (row >> shift) == (col >> shift)
    gap = (row - col) & (across - 1)
    beside = jnp.where((gap == 1) | (gap == across - 1), 1.0, 0.0)
    middle = jnp.where(gap == 0, 3.0, 0.0)
    left = jnp.where(same, beside + middle - 1.5 / across, 0.0).astype(BF16)
    half = width // 2
    source, level = iota((width, 2 * width), 0), iota((width, 2 * width), 1)
    inside = (source < half) == (level < half)
    near = jnp.where(jnp.abs(source - level) == 1, 0.75, 0.0)
    edge = (level == 0) | (level == half - 1) | (level == half) | (level == width - 1)
    near = near - jnp.where(source == level, jnp.where(edge, 0.75, 1.5), 0.0)
    vertical = jnp.where(inside, near, 0.0)
    target = level - width
    sign = jnp.where(target < half, 1.0, -1.0)
    of_level = (source & (half - 1)) == (target & (half - 1))
    phase = jnp.where(of_level, jnp.where(source < half, -0.5, 1.0) * sign, 0.0)
    right = jnp.where(level < width, vertical, phase).astype(BF16)
    rows = iota((GROUP, size), 0)
    total = ones_where(rows == (iota((GROUP, size), 1) >> shift))
    return left, right, total


def steps(states, forcings, counts, left, right, across, width):
    size = GROUP * across
    spread = lambda rows: jnp.broadcast_to(rows[:, None, :], (GROUP, across, width)).reshape(size, width)
    states = list(states)
    for least in (0.5, 1.5):
        linear = [fast(left, state) for state in states]
        levels = [fast(state, right) for state in states]
        moved = [
            0.2 * (a + b[:, :width] + spread(1.5 * f)) + 0.25 * jnp.tanh(b[:, width:])
            for a, b, f in zip(linear, levels, forcings)
        ]
        states = [
            jnp.where(spread(count) > least, new, old.astype(F32)).astype(BF16)
            for new, old, count in zip(moved, states, counts)
        ]
    return states


def kernel(n, cap, capp, mcap,
           gcm_hbm, cloud_hbm, owner_hbm, substeps_hbm, neigh_hbm, slot_hbm, dest_hbm,
           new_hbm, crm_hbm, arrived_ref,
           gcm_ref, owner_ref, substeps_ref, neigh_ref, slot_ref, dest_ref, new_ref, crm_ref, ext, dyn, fsend, frecv, fc, fbatch, keep, tend, tsend, trecv, work, depart,
           landed, notes, noted, pick_v, pick,
           halo_send, halo_recv, f_send, f_recv, t_send, t_recv, m_send, m_recv, own_sem,
           in_sem, cloud_sem, pick_sem, out_sem,
           r_send, r_recv, g_send, g_recv, l_sem):
    me = lax.axis_index("col")
    cols, width = gcm_hbm.shape
    slots, across, _ = cloud_hbm.shape
    listed = slot_hbm.shape[1]
    elements = cols // 9
    margin = elements // 2
    table = n * capp
    spots = n * mcap
    shift = capp.bit_length() - 1
    right_dev, left_dev = lax.rem(me + 1, n), lax.rem(me + n - 1, n)

    inputs = [
        pltpu.make_async_copy(source, target, in_sem.at[i])
        for i, (source, target) in enumerate([
            (gcm_hbm, gcm_ref), (owner_hbm, owner_ref), (substeps_hbm, substeps_ref),
            (neigh_hbm, neigh_ref), (slot_hbm, slot_ref), (dest_hbm, dest_ref)])
    ]
    for copy in inputs:
        copy.start()
    cloud_copy = pltpu.make_async_copy(cloud_hbm, work.at[pl.ds(0, slots)], cloud_sem)
    cloud_copy.start()
    barrier = pltpu.get_barrier_semaphore()

    def greet(k, carry):
        pl.semaphore_signal(barrier, inc=1, device_id={"col": lax.rem(me + k, n)}, device_id_type=MESH)
        return carry

    lax.fori_loop(1, n, greet, 0)

    for copy in inputs:
        copy.wait()
    gcm = gcm_ref[...]
    place = iota((elements, cols), 1) - 9 * iota((elements, cols), 0)
    member = ones_where((place >= 0) & (place < 9), F32)
    means = exact(member, gcm) * (1.0 / 9.0)
    ext[pl.ds(margin, elements), :] = means
    pl.semaphore_wait(barrier, n - 1)

    up = pltpu.make_async_remote_copy(
        src_ref=ext.at[pl.ds(elements, margin)], dst_ref=ext.at[pl.ds(0, margin)],
        send_sem=halo_send.at[0], recv_sem=halo_recv.at[0],
        device_id={"col": right_dev}, device_id_type=MESH)
    down = pltpu.make_async_remote_copy(
        src_ref=ext.at[pl.ds(margin, margin)], dst_ref=ext.at[pl.ds(margin + elements, margin)],
        send_sem=halo_send.at[1], recv_sem=halo_recv.at[1],
        device_id={"col": left_dev}, device_id_type=MESH)
    up.start()
    down.start()

    slot_row, dest_row = slot_ref[...], dest_ref[...]
    slot_col = jnp.broadcast_to(slot_row, (listed, listed)).T
    dest_col = jnp.broadcast_to(dest_row, (listed, listed)).T
    same = (dest_col == dest_row) & (iota((listed, listed), 1) < iota((listed, listed), 0))
    place_mig = dest_col[:, 0:1] * mcap + jnp.sum(jnp.where(same, 1, 0), axis=1, keepdims=True)
    found = iota((listed, spots), 1) == place_mig
    chosen = jnp.sum(jnp.where(found, slot_col[:, 0:1] - slots, 0), axis=0, keepdims=True) + slots
    pick_v[...] = chosen
    pick_copy = pltpu.make_async_copy(pick_v, pick, pick_sem)
    pick_copy.start()
    work[pl.ds(slots, 1)] = jnp.zeros((1, across, width), BF16)
    pick_copy.wait()
    cloud_copy.wait()

    def partner(j):
        half = lax.div(j + 1, 2)
        return n // 2 + jnp.where(lax.rem(j, 2) == 1, -half, half)

    def mig_copy(j):
        k = partner(j)
        return pltpu.make_async_remote_copy(
            src_ref=depart.at[pl.ds(j * mcap, mcap)],
            dst_ref=arrived_ref.at[pl.ds(me * mcap, mcap)],
            send_sem=m_send.at[k], recv_sem=m_recv.at[k],
            device_id={"col": lax.rem(me + k, n)}, device_id_type=MESH)

    per_batch = max(1, BATCH // mcap)
    raw = RAW * per_batch

    def raw_copy(j):
        return pltpu.make_async_remote_copy(
            src_ref=depart.at[pl.ds(j * mcap, mcap)], dst_ref=landed.at[pl.ds(j * mcap, mcap)],
            send_sem=r_send.at[j], recv_sem=r_recv.at[j],
            device_id={"col": lax.rem(me + partner(j), n)}, device_id_type=MESH)

    def pack(j, dest):
        for r in range(mcap):
            depart[j * mcap + r] = work[pick[0, dest * mcap + r]]

    def raw_body(j, carry):
        pack(j, lax.rem(me + partner(j), n))
        raw_copy(j).start()
        return carry

    lax.fori_loop(0, raw // 2, raw_body, 0)

    owner_row = owner_ref[...]
    hits = iota((n, cols), 0) == owner_row
    earlier = ones_where(iota((cols, cols), 0) < iota((cols, cols), 1))
    before = fast(ones_where(hits), earlier)
    rank = jnp.sum(jnp.where(hits, before, 0.0), axis=0, keepdims=True).astype(I32)
    place_row = owner_row * capp + rank
    scatter = ones_where(iota((table, cols), 0) == place_row)
    p_col = iota((table, cols), 0)
    count_row = ones_where(((p_col & (capp - 1)) == cap) & ((p_col >> shift) == owner_row))
    count_lane = jnp.where(iota((width, cols), 0) == rank, substeps_ref[...].astype(F32), 0.0).astype(BF16)
    sent_counts = lax.dot_general(count_row, count_lane, (((1,), (1,)), ((), ())), preferred_element_type=F32)
    fsend[...] = sent_counts.astype(BF16).reshape(n, capp, width)

    ids = neigh_ref[...] - me * elements + margin
    span = elements * n
    ids = jnp.where(ids < 0, ids + span, ids)
    ids = jnp.where(ids >= span, ids - span, ids)
    tall = iota((elements + 2 * margin, elements), 0)
    weights = jnp.where(tall == iota((elements + 2 * margin, elements), 1) + margin, -4.0, 0.0)
    for k in range(neigh_ref.shape[0]):
        weights = weights + jnp.where(tall == ids[k:k + 1, :], 1.0, 0.0)
    spread_gap = iota((cols, elements), 0) - 9 * iota((cols, elements), 1)
    spread = ones_where((spread_gap >= 0) & (spread_gap < 9), F32)
    per_column = fast(spread.astype(BF16), weights.T.astype(BF16))

    up.wait()
    down.wait()
    state = gcm + 0.2 * exact(per_column, ext[...])
    dyn[...] = state
    sent = fast(scatter, state.astype(BF16)) + fsend[...].reshape(table, width).astype(F32)
    fsend[...] = sent.astype(BF16).reshape(n, capp, width)

    def forcing_copy(k):
        return pltpu.make_async_remote_copy(
            src_ref=fsend.at[lax.rem(me + k, n)], dst_ref=frecv.at[me],
            send_sem=f_send.at[k], recv_sem=f_recv.at[k],
            device_id={"col": lax.rem(me + k, n)}, device_id_type=MESH)

    def start(copy):
        def body(k, carry):
            copy(k).start()
            return carry
        lax.fori_loop(1, n, body, 0)

    def wait_recv(copy):
        def body(k, carry):
            copy(k).wait_recv()
            return carry
        lax.fori_loop(1, n, body, 0)

    def wait_send(copy):
        def body(k, carry):
            copy(k).wait_send()
            return carry
        lax.fori_loop(1, n, body, 0)

    start(forcing_copy)
    lax.fori_loop(raw // 2, raw, raw_body, 0)
    frecv[me] = fsend[me]

    gone = iota((slots, listed), 0) == slot_ref[...]
    gone = jnp.max(jnp.where(gone, 1.0, 0.0), axis=1, keepdims=True)
    keep[...] = jnp.broadcast_to(1.0 - gone, (slots, width))
    fc[pl.ds(slots, 8), :] = jnp.zeros((8, 2 * width), F32)
    left, right, total = step_matrices(across, width)
    p_lane = iota((slots, table), 1)
    q_lane = (p_lane >> shift) * cap + (p_lane & (capp - 1))
    compact = ones_where((q_lane == iota((slots, table), 0)) & ((p_lane & (capp - 1)) < cap))
    first = (p_lane >> shift) * cap
    q_table = iota((slots, table), 0)
    counting = ones_where(((p_lane & (capp - 1)) == cap) & (q_table >= first) & (q_table < first + cap))
    within = fast(compact, ones_where((iota((table, width), 0) & (capp - 1)) == iota((table, width), 1)))

    wait_recv(forcing_copy)
    received = frecv[...].reshape(table, width)
    fc[pl.ds(0, slots), 0:width] = fast(compact, received)
    count = jnp.sum(fast(counting, received) * within, axis=1, keepdims=True)
    fc[pl.ds(0, slots), width:2 * width] = jnp.broadcast_to(count, (slots, width))

    early = (RAW + EARLY) * per_batch
    size = GROUP * across

    def note_copy(j):
        return pltpu.make_async_remote_copy(
            src_ref=notes.at[j], dst_ref=noted.at[j],
            send_sem=g_send.at[j], recv_sem=g_recv.at[j],
            device_id={"col": lax.rem(me + partner(j), n)}, device_id_type=MESH)

    def note_body(b, carry):
        for i in range(BATCH):
            j = b * per_batch + i // mcap
            at = pick[0, lax.rem(me + partner(j), n) * mcap + i % mcap]
            fbatch[i:i + 1, :] = fc[pl.ds(at, 1), :]
        forcing, count = fbatch[:, 0:width], fbatch[:, width:2 * width]
        row, lane = iota((BATCH, width), 0), iota((BATCH, width), 1)
        for g in range(per_batch):
            mine = (row >= g * mcap) & (row < (g + 1) * mcap)
            line = jnp.sum(jnp.where(mine & (row == lane), count, 0.0), axis=0, keepdims=True)
            lower = jnp.where(row == 0, jnp.broadcast_to(line, (BATCH, width)), 0.0)
            notes[b * per_batch + g] = jnp.concatenate(
                [jnp.where(mine, forcing, 0.0), lower], axis=0).astype(BF16)
            note_copy(b * per_batch + g).start()
        return carry

    lax.fori_loop(0, RAW, note_body, 0)

    def early_body(b, carry):
        for i in range(BATCH):
            j = b * per_batch + i // mcap
            at = pick[0, lax.rem(me + partner(j), n) * mcap + i % mcap]
            depart[b * BATCH + i] = work[at]
            fbatch[i:i + 1, :] = fc[pl.ds(at, 1), :]
        forcings, counts, states = [], [], []
        for g in range(BATCH // GROUP):
            states.append(depart[pl.ds(b * BATCH + g * GROUP, GROUP)].reshape(size, width))
            forcings.append(fbatch[g * GROUP:(g + 1) * GROUP, 0:width])
            counts.append(fbatch[g * GROUP:(g + 1) * GROUP, width:2 * width])
        finals = steps(states, forcings, counts, left, right, across, width)
        for g, final in enumerate(finals):
            depart[pl.ds(b * BATCH + g * GROUP, GROUP)] = final.reshape(GROUP, across, width)
        for j in range(per_batch):
            mig_copy(b * per_batch + j).start()
        return carry

    lax.fori_loop(RAW, RAW + EARLY, early_body, 0)

    def chunk(c, carry):
        rows = [pl.ds(pl.multiple_of((c * TOGETHER + g) * GROUP, GROUP), GROUP) for g in range(TOGETHER)]
        forcings = [fc[row, 0:width] for row in rows]
        counts = [fc[row, width:2 * width] for row in rows]
        stays = [keep[row, :] for row in rows]
        begins = [work[row].reshape(size, width) for row in rows]
        finals = steps(begins, forcings, counts, left, right, across, width)
        gains = [fast(total, final) - fast(total, begin) for final, begin in zip(finals, begins)]
        for row, final, gain, count, stay in zip(rows, finals, gains, counts, stays):
            tend[row, :] = gain * (1.0 / across) / jnp.maximum(count, 1.0)
            work[row] = final.reshape(GROUP, across, width)
            stay = jnp.broadcast_to(stay[:, None, :], (GROUP, across, width)).astype(BF16)
            crm_ref[row] = final.reshape(GROUP, across, width) * stay
        return carry

    lax.fori_loop(0, slots // (GROUP * TOGETHER), chunk, 0)

    p_row = iota((table, slots), 0)
    q_row = (p_row >> shift) * cap + (p_row & (capp - 1))
    expand = ones_where((q_row == iota((table, slots), 1)) & ((p_row & (capp - 1)) < cap))
    tsend[...] = fast(expand, tend[...].astype(BF16)).astype(BF16).reshape(n, capp, width)

    def tendency_copy(k):
        return pltpu.make_async_remote_copy(
            src_ref=tsend.at[lax.rem(me + k, n)], dst_ref=trecv.at[me],
            send_sem=t_send.at[k], recv_sem=t_recv.at[k],
            device_id={"col": lax.rem(me + k, n)}, device_id_type=MESH)

    start(tendency_copy)
    trecv[me] = tsend[me]

    def depart_body(j, carry):
        pack(j, lax.rem(me + partner(j), n))
        mig_copy(j).start()
        return carry

    lax.fori_loop(early, n - 1, depart_body, 0)
    pack(n - 1, me)
    own = pltpu.make_async_copy(
        depart.at[pl.ds((n - 1) * mcap, mcap)], arrived_ref.at[pl.ds(me * mcap, mcap)], own_sem)
    own.start()

    def landed_copy(j):
        source = lax.rem(me - partner(j) + n, n)
        return pltpu.make_async_copy(
            landed.at[pl.ds(j * mcap, mcap)], arrived_ref.at[pl.ds(source * mcap, mcap)], l_sem.at[j])

    def landed_body(b, carry):
        note = jnp.zeros((2 * BATCH, width), F32)
        for g in range(per_batch):
            raw_copy(b * per_batch + g).wait_recv()
            note_copy(b * per_batch + g).wait_recv()
            note = note + noted[b * per_batch + g].astype(F32)
        row, lane = iota((BATCH, width), 0), iota((BATCH, width), 1)
        line = jnp.broadcast_to(note[BATCH:BATCH + 1, :], (BATCH, width))
        count = jnp.sum(jnp.where(row == lane, line, 0.0), axis=1, keepdims=True)
        count = jnp.broadcast_to(count, (BATCH, width))
        parts = [slice(g * GROUP, (g + 1) * GROUP) for g in range(BATCH // GROUP)]
        places = [pl.ds(b * BATCH + g * GROUP, GROUP) for g in range(BATCH // GROUP)]
        finals = steps(
            [landed[at].reshape(size, width) for at in places], [note[part] for part in parts],
            [count[part] for part in parts], left, right, across, width)
        for at, final in zip(places, finals):
            landed[at] = final.reshape(GROUP, across, width)
        for g in range(per_batch):
            landed_copy(b * per_batch + g).start()
        return carry

    lax.fori_loop(0, RAW, landed_body, 0)

    crm_copy = pltpu.make_async_copy(crm_ref, crm_hbm, out_sem.at[0])
    crm_copy.start()
    wait_recv(tendency_copy)
    back = lax.dot_general(
        scatter, trecv[...].reshape(table, width), (((0,), (0,)), ((), ())), preferred_element_type=F32)
    new_ref[...] = dyn[...] + back
    new_copy = pltpu.make_async_copy(new_ref, new_hbm, out_sem.at[1])
    new_copy.start()

    wait_send(forcing_copy)
    wait_send(tendency_copy)

    def finish(j, carry):
        mig_copy(j).wait()
        return carry

    lax.fori_loop(raw, n - 1, finish, 0)

    def finish_raw(j, carry):
        raw_copy(j).wait_send()
        note_copy(j).wait_send()
        landed_copy(j).wait()
        return carry

    lax.fori_loop(0, raw, finish_raw, 0)
    own.wait()
    crm_copy.wait()
    new_copy.wait()


def store(*refs):
    count = (len(refs) - 2) // 3
    sources, targets, stages = refs[:count], refs[count:2 * count], refs[2 * count:3 * count]
    sems_in, sems_out = refs[-2:]
    reads, writes = [], []
    for source, target, stage in zip(sources, targets, stages):
        parts = 1 if len(source.shape) == 2 else PIECES
        rows = source.shape[0] // parts
        for i in range(parts):
            at, sem = pl.ds(i * rows, rows), len(reads)
            reads.append(pltpu.make_async_copy(source.at[at], stage.at[at], sems_in.at[sem]))
            writes.append(pltpu.make_async_copy(stage.at[at], target.at[at], sems_out.at[sem]))
    for read in reads:
        read.start()
    for read, write in zip(reads, writes):
        read.wait()
        write.start()
    for write in writes:
        write.wait()


def per_device(gcm_state, cloud_model_state, owner, substeps, neighbours, mig_slot, mig_dest):
    n = lax.axis_size("col")
    cols, width = gcm_state.shape
    slots, across, _ = cloud_model_state.shape
    cap = slots // n
    capp = 16
    while capp <= cap:
        capp *= 2
    listed = mig_slot.shape[0]
    mcap = max(2, 2 * listed // n)
    elements = cols // 9
    hbm = pl.BlockSpec(memory_space=pltpu.HBM)
    anywhere = pl.BlockSpec(memory_space=pl.ANY)
    dma = pltpu.SemaphoreType.DMA
    table = n * capp
    raw = RAW * max(1, BATCH // mcap)
    results = pl.pallas_call(
        functools.partial(kernel, n, cap, capp, mcap),
        out_shape=(
            jax.ShapeDtypeStruct((cols, width), F32),
            jax.ShapeDtypeStruct((slots, across, width), BF16),
            jax.ShapeDtypeStruct((n * mcap, across, width), BF16),
        ),
        in_specs=[hbm] * 7,
        out_specs=(hbm, hbm, hbm),
        scratch_shapes=[
            pltpu.VMEM((cols, width), F32),
            pltpu.VMEM((1, cols), I32),
            pltpu.VMEM((1, cols), I32),
            pltpu.VMEM(neighbours.shape[::-1], I32),
            pltpu.VMEM((1, listed), I32),
            pltpu.VMEM((1, listed), I32),
            pltpu.VMEM((cols, width), F32),
            pltpu.VMEM((slots, across, width), BF16),
            pltpu.VMEM((2 * elements, width), F32),
            pltpu.VMEM((cols, width), F32),
            pltpu.VMEM((n, capp, width), BF16),
            pltpu.VMEM((n, capp, width), BF16),
            pltpu.VMEM((slots + 8, 2 * width), F32),
            pltpu.VMEM((BATCH, 2 * width), F32),
            pltpu.VMEM((slots, width), F32),
            pltpu.VMEM((slots, width), F32),
            pltpu.VMEM((n, capp, width), BF16),
            pltpu.VMEM((n, capp, width), BF16),
            pltpu.VMEM((slots + 1, across, width), BF16),
            pltpu.VMEM((n * mcap, across, width), BF16),
            pltpu.VMEM((raw * mcap, across, width), BF16),
            pltpu.VMEM((raw, 2 * BATCH, width), BF16),
            pltpu.VMEM((raw, 2 * BATCH, width), BF16),
            pltpu.VMEM((1, n * mcap), I32),
            pltpu.SMEM((1, n * mcap), I32),
            dma((2,)), dma((2,)), dma((n,)), dma((n,)), dma((n,)), dma((n,)), dma((n,)), dma((n,)),
            dma, dma((6,)), dma, dma, dma((2,)),
            dma((raw,)), dma((raw,)), dma((raw,)), dma((raw,)), dma((raw,)),
        ],
        compiler_params=pltpu.CompilerParams(
            collective_id=0, has_side_effects=True, vmem_limit_bytes=56 * 1024 * 1024),
        cost_estimate=pl.CostEstimate(flops=5 * 10**9, bytes_accessed=10**7, transcendentals=2 * 10**6),
    )(
        gcm_state, cloud_model_state, owner.reshape(1, cols), substeps.reshape(1, cols),
        neighbours.T, mig_slot.reshape(1, listed), mig_dest.reshape(1, listed),
    )
    return pl.pallas_call(
        store,
        out_shape=tuple(jax.ShapeDtypeStruct(r.shape, r.dtype) for r in results),
        in_specs=[anywhere] * 3, out_specs=(anywhere,) * 3,
        scratch_shapes=[pltpu.VMEM(r.shape, r.dtype) for r in results] + [dma((1 + 2 * PIECES,))] * 2,
        compiler_params=pltpu.CompilerParams(vmem_limit_bytes=56 * 1024 * 1024),
    )(*results)


def solution(mesh):
    wide, deep, flat = P(("ens", "col"), None), P(("ens", "col"), None, None), P(("ens", "col"))
    return jax.shard_map(
        per_device, mesh=mesh,
        in_specs=(wide, deep, wide, flat, wide, flat, wide),
        out_specs=(wide, deep, deep), check_vma=False,
    )
```

```python
import functools

import jax
import jax.numpy as jnp
from jax import lax
from jax.experimental import pallas as pl
from jax.experimental.pallas import tpu as pltpu
from jax.sharding import PartitionSpec as P

F32, BF16, I32 = jnp.float32, jnp.bfloat16, jnp.int32
MESH = pl.DeviceIdType.MESH
GROUP = 8
TOGETHER = 4
BATCH = 16
EARLY = 3
PIECES = 2
RAW = 2


def iota(shape, dim):
    return lax.broadcasted_iota(I32, shape, dim)


def ones_where(condition, dtype=BF16):
    return jnp.where(condition, 1.0, 0.0).astype(dtype)


def exact(a, b):
    return jnp.dot(a, b, preferred_element_type=F32, precision=lax.Precision.HIGHEST)


def fast(a, b):
    return jnp.dot(a, b, preferred_element_type=F32)


def step_matrices(across, width):
    size = GROUP * across
    shift = across.bit_length() - 1
    row, col = iota((size, size), 0), iota((size, size), 1)
    same = (row >> shift) == (col >> shift)
    gap = (row - col) & (across - 1)
    beside = jnp.where((gap == 1) | (gap == across - 1), 1.0, 0.0)
    middle = jnp.where(gap == 0, 3.0, 0.0)
    left = jnp.where(same, beside + middle - 1.5 / across, 0.0).astype(BF16)
    half = width // 2
    source, level = iota((width, 2 * width), 0), iota((width, 2 * width), 1)
    inside = (source < half) == (level < half)
    near = jnp.where(jnp.abs(source - level) == 1, 0.75, 0.0)
    edge = (level == 0) | (level == half - 1) | (level == half) | (level == width - 1)
    near = near - jnp.where(source == level, jnp.where(edge, 0.75, 1.5), 0.0)
    vertical = jnp.where(inside, near, 0.0)
    target = level - width
    sign = jnp.where(target < half, 1.0, -1.0)
    of_level = (source & (half - 1)) == (target & (half - 1))
    phase = jnp.where(of_level, jnp.where(source < half, -0.5, 1.0) * sign, 0.0)
    right = jnp.where(level < width, vertical, phase).astype(BF16)
    rows = iota((GROUP, size), 0)
    total = ones_where(rows == (iota((GROUP, size), 1) >> shift))
    return left, right, total


def steps(states, forcings, counts, left, right, across, width):
    size = GROUP * across
    spread = lambda rows: jnp.broadcast_to(rows[:, None, :], (GROUP, across, width)).reshape(size, width)
    states = list(states)
    for least in (0.5, 1.5):
        linear = [fast(left, state) for state in states]
        levels = [fast(state, right) for state in states]
        moved = [
            0.2 * (a + b[:, :width] + spread(1.5 * f)) + 0.25 * jnp.tanh(b[:, width:])
            for a, b, f in zip(linear, levels, forcings)
        ]
        states = [
            jnp.where(spread(count) > least, new, old.astype(F32)).astype(BF16)
            for new, old, count in zip(moved, states, counts)
        ]
    return states


def kernel(n, cap, capp, mcap,
           gcm_hbm, cloud_hbm, owner_hbm, substeps_hbm, neigh_hbm, slot_hbm, dest_hbm,
           new_hbm, crm_hbm, arrived_ref,
           gcm_ref, owner_ref, substeps_ref, neigh_ref, slot_ref, dest_ref, new_ref, crm_ref, ext, dyn, fsend, frecv, fc, fbatch, keep, tend, tsend, trecv, work, depart,
           landed, notes, noted, pick_v, pick,
           halo_send, halo_recv, f_send, f_recv, t_send, t_recv, m_send, m_recv, own_sem,
           in_sem, cloud_sem, pick_sem, out_sem,
           r_send, r_recv, g_send, g_recv, l_sem):
    me = lax.axis_index("col")
    cols, width = gcm_hbm.shape
    slots, across, _ = cloud_hbm.shape
    listed = slot_hbm.shape[1]
    elements = cols // 9
    margin = elements // 2
    table = n * capp
    spots = n * mcap
    shift = capp.bit_length() - 1
    right_dev, left_dev = lax.rem(me + 1, n), lax.rem(me + n - 1, n)

    inputs = [
        pltpu.make_async_copy(source, target, in_sem.at[i])
        for i, (source, target) in enumerate([
            (gcm_hbm, gcm_ref), (owner_hbm, owner_ref), (substeps_hbm, substeps_ref),
            (neigh_hbm, neigh_ref), (slot_hbm, slot_ref), (dest_hbm, dest_ref)])
    ]
    for copy in inputs:
        copy.start()
    cloud_copy = pltpu.make_async_copy(cloud_hbm, work.at[pl.ds(0, slots)], cloud_sem)
    cloud_copy.start()
    barrier = pltpu.get_barrier_semaphore()

    def greet(k, carry):
        pl.semaphore_signal(barrier, inc=1, device_id={"col": lax.rem(me + k, n)}, device_id_type=MESH)
        return carry

    lax.fori_loop(1, n, greet, 0)

    for copy in inputs:
        copy.wait()
    gcm = gcm_ref[...]
    place = iota((elements, cols), 1) - 9 * iota((elements, cols), 0)
    member = ones_where((place >= 0) & (place < 9), F32)
    means = exact(member, gcm) * (1.0 / 9.0)
    ext[pl.ds(margin, elements), :] = means
    slot_row, dest_row = slot_ref[...], dest_ref[...]
    slot_col = jnp.broadcast_to(slot_row, (listed, listed)).T
    dest_col = jnp.broadcast_to(dest_row, (listed, listed)).T
    same = (dest_col == dest_row) & (iota((listed, listed), 1) < iota((listed, listed), 0))
    place_mig = dest_col[:, 0:1] * mcap + jnp.sum(jnp.where(same, 1, 0), axis=1, keepdims=True)
    found = iota((listed, spots), 1) == place_mig
    chosen = jnp.sum(jnp.where(found, slot_col[:, 0:1] - slots, 0), axis=0, keepdims=True) + slots
    pick_v[...] = chosen
    pick_copy = pltpu.make_async_copy(pick_v, pick, pick_sem)
    pick_copy.start()
    work[pl.ds(slots, 1)] = jnp.zeros((1, across, width), BF16)
    pick_copy.wait()
    cloud_copy.wait()
    pl.semaphore_wait(barrier, n - 1)

    up = pltpu.make_async_remote_copy(
        src_ref=ext.at[pl.ds(elements, margin)], dst_ref=ext.at[pl.ds(0, margin)],
        send_sem=halo_send.at[0], recv_sem=halo_recv.at[0],
        device_id={"col": right_dev}, device_id_type=MESH)
    down = pltpu.make_async_remote_copy(
        src_ref=ext.at[pl.ds(margin, margin)], dst_ref=ext.at[pl.ds(margin + elements, margin)],
        send_sem=halo_send.at[1], recv_sem=halo_recv.at[1],
        device_id={"col": left_dev}, device_id_type=MESH)
    up.start()
    down.start()

    def partner(j):
        half = lax.div(j + 1, 2)
        return n // 2 + jnp.where(lax.rem(j, 2) == 1, -half, half)

    def mig_copy(j):
        k = partner(j)
        return pltpu.make_async_remote_copy(
            src_ref=depart.at[pl.ds(j * mcap, mcap)],
            dst_ref=arrived_ref.at[pl.ds(me * mcap, mcap)],
            send_sem=m_send.at[k], recv_sem=m_recv.at[k],
            device_id={"col": lax.rem(me + k, n)}, device_id_type=MESH)

    per_batch = max(1, BATCH // mcap)
    raw = RAW * per_batch

    def raw_copy(j):
        return pltpu.make_async_remote_copy(
            src_ref=depart.at[pl.ds(j * mcap, mcap)], dst_ref=landed.at[pl.ds(j * mcap, mcap)],
            send_sem=r_send.at[j], recv_sem=r_recv.at[j],
            device_id={"col": lax.rem(me + partner(j), n)}, device_id_type=MESH)

    def pack(j, dest):
        for r in range(mcap):
            depart[j * mcap + r] = work[pick[0, dest * mcap + r]]

    def raw_body(j, carry):
        pack(j, lax.rem(me + partner(j), n))
        raw_copy(j).start()
        return carry

    lax.fori_loop(0, raw // 2, raw_body, 0)

    owner_row = owner_ref[...]
    hits = iota((n, cols), 0) == owner_row
    earlier = ones_where(iota((cols, cols), 0) < iota((cols, cols), 1))
    before = fast(ones_where(hits), earlier)
    rank = jnp.sum(jnp.where(hits, before, 0.0), axis=0, keepdims=True).astype(I32)
    place_row = owner_row * capp + rank
    scatter = ones_where(iota((table, cols), 0) == place_row)
    p_col = iota((table, cols), 0)
    count_row = ones_where(((p_col & (capp - 1)) == cap) & ((p_col >> shift) == owner_row))
    count_lane = jnp.where(iota((width, cols), 0) == rank, substeps_ref[...].astype(F32), 0.0).astype(BF16)
    sent_counts = lax.dot_general(count_row, count_lane, (((1,), (1,)), ((), ())), preferred_element_type=F32)
    fsend[...] = sent_counts.astype(BF16).reshape(n, capp, width)

    ids = neigh_ref[...] - me * elements + margin
    span = elements * n
    ids = jnp.where(ids < 0, ids + span, ids)
    ids = jnp.where(ids >= span, ids - span, ids)
    tall = iota((elements + 2 * margin, elements), 0)
    weights = jnp.where(tall == iota((elements + 2 * margin, elements), 1) + margin, -4.0, 0.0)
    for k in range(neigh_ref.shape[0]):
        weights = weights + jnp.where(tall == ids[k:k + 1, :], 1.0, 0.0)
    spread_gap = iota((cols, elements), 0) - 9 * iota((cols, elements), 1)
    spread = ones_where((spread_gap >= 0) & (spread_gap < 9), F32)
    per_column = fast(spread.astype(BF16), weights.T.astype(BF16))

    up.wait()
    down.wait()
    state = gcm + 0.2 * exact(per_column, ext[...])
    dyn[...] = state
    sent = fast(scatter, state.astype(BF16)) + fsend[...].reshape(table, width).astype(F32)
    fsend[...] = sent.astype(BF16).reshape(n, capp, width)

    def forcing_copy(k):
        return pltpu.make_async_remote_copy(
            src_ref=fsend.at[lax.rem(me + k, n)], dst_ref=frecv.at[me],
            send_sem=f_send.at[k], recv_sem=f_recv.at[k],
            device_id={"col": lax.rem(me + k, n)}, device_id_type=MESH)

    def start(copy):
        def body(k, carry):
            copy(k).start()
            return carry
        lax.fori_loop(1, n, body, 0)

    def wait_recv(copy):
        def body(k, carry):
            copy(k).wait_recv()
            return carry
        lax.fori_loop(1, n, body, 0)

    def wait_send(copy):
        def body(k, carry):
            copy(k).wait_send()
            return carry
        lax.fori_loop(1, n, body, 0)

    start(forcing_copy)
    lax.fori_loop(raw // 2, raw, raw_body, 0)
    frecv[me] = fsend[me]

    gone = iota((slots, listed), 0) == slot_ref[...]
    gone = jnp.max(jnp.where(gone, 1.0, 0.0), axis=1, keepdims=True)
    keep[...] = jnp.broadcast_to(1.0 - gone, (slots, width))
    fc[pl.ds(slots, 8), :] = jnp.zeros((8, 2 * width), F32)
    left, right, total = step_matrices(across, width)
    p_lane = iota((slots, table), 1)
    q_lane = (p_lane >> shift) * cap + (p_lane & (capp - 1))
    compact = ones_where((q_lane == iota((slots, table), 0)) & ((p_lane & (capp - 1)) < cap))
    first = (p_lane >> shift) * cap
    q_table = iota((slots, table), 0)
    counting = ones_where(((p_lane & (capp - 1)) == cap) & (q_table >= first) & (q_table < first + cap))
    within = fast(compact, ones_where((iota((table, width), 0) & (capp - 1)) == iota((table, width), 1)))

    wait_recv(forcing_copy)
    received = frecv[...].reshape(table, width)
    fc[pl.ds(0, slots), 0:width] = fast(compact, received)
    count = jnp.sum(fast(counting, received) * within, axis=1, keepdims=True)
    fc[pl.ds(0, slots), width:2 * width] = jnp.broadcast_to(count, (slots, width))

    early = (RAW + EARLY) * per_batch
    size = GROUP * across

    def note_copy(j):
        return pltpu.make_async_remote_copy(
            src_ref=notes.at[j], dst_ref=noted.at[j],
            send_sem=g_send.at[j], recv_sem=g_recv.at[j],
            device_id={"col": lax.rem(me + partner(j), n)}, device_id_type=MESH)

    def note_body(b, carry):
        for i in range(BATCH):
            j = b * per_batch + i // mcap
            at = pick[0, lax.rem(me + partner(j), n) * mcap + i % mcap]
            fbatch[i:i + 1, :] = fc[pl.ds(at, 1), :]
        forcing, count = fbatch[:, 0:width], fbatch[:, width:2 * width]
        row, lane = iota((BATCH, width), 0), iota((BATCH, width), 1)
        for g in range(per_batch):
            mine = (row >= g * mcap) & (row < (g + 1) * mcap)
            line = jnp.sum(jnp.where(mine & (row == lane), count, 0.0), axis=0, keepdims=True)
            lower = jnp.where(row == 0, jnp.broadcast_to(line, (BATCH, width)), 0.0)
            notes[b * per_batch + g] = jnp.concatenate(
                [jnp.where(mine, forcing, 0.0), lower], axis=0).astype(BF16)
            note_copy(b * per_batch + g).start()
        return carry

    lax.fori_loop(0, RAW, note_body, 0)

    def early_body(b, carry):
        for i in range(BATCH):
            j = b * per_batch + i // mcap
            at = pick[0, lax.rem(me + partner(j), n) * mcap + i % mcap]
            depart[b * BATCH + i] = work[at]
            fbatch[i:i + 1, :] = fc[pl.ds(at, 1), :]
        forcings, counts, states = [], [], []
        for g in range(BATCH // GROUP):
            states.append(depart[pl.ds(b * BATCH + g * GROUP, GROUP)].reshape(size, width))
            forcings.append(fbatch[g * GROUP:(g + 1) * GROUP, 0:width])
            counts.append(fbatch[g * GROUP:(g + 1) * GROUP, width:2 * width])
        finals = steps(states, forcings, counts, left, right, across, width)
        for g, final in enumerate(finals):
            depart[pl.ds(b * BATCH + g * GROUP, GROUP)] = final.reshape(GROUP, across, width)
        for j in range(per_batch):
            mig_copy(b * per_batch + j).start()
        return carry

    lax.fori_loop(RAW, RAW + EARLY, early_body, 0)

    def chunk(c, carry):
        rows = [pl.ds(pl.multiple_of((c * TOGETHER + g) * GROUP, GROUP), GROUP) for g in range(TOGETHER)]
        forcings = [fc[row, 0:width] for row in rows]
        counts = [fc[row, width:2 * width] for row in rows]
        stays = [keep[row, :] for row in rows]
        begins = [work[row].reshape(size, width) for row in rows]
        finals = steps(begins, forcings, counts, left, right, across, width)
        gains = [fast(total, final) - fast(total, begin) for final, begin in zip(finals, begins)]
        for row, final, gain, count, stay in zip(rows, finals, gains, counts, stays):
            tend[row, :] = gain * (1.0 / across) / jnp.maximum(count, 1.0)
            work[row] = final.reshape(GROUP, across, width)
            stay = jnp.broadcast_to(stay[:, None, :], (GROUP, across, width)).astype(BF16)
            crm_ref[row] = final.reshape(GROUP, across, width) * stay
        return carry

    lax.fori_loop(0, slots // (GROUP * TOGETHER), chunk, 0)

    p_row = iota((table, slots), 0)
    q_row = (p_row >> shift) * cap + (p_row & (capp - 1))
    expand = ones_where((q_row == iota((table, slots), 1)) & ((p_row & (capp - 1)) < cap))
    tsend[...] = fast(expand, tend[...].astype(BF16)).astype(BF16).reshape(n, capp, width)

    def tendency_copy(k):
        return pltpu.make_async_remote_copy(
            src_ref=tsend.at[lax.rem(me + k, n)], dst_ref=trecv.at[me],
            send_sem=t_send.at[k], recv_sem=t_recv.at[k],
            device_id={"col": lax.rem(me + k, n)}, device_id_type=MESH)

    start(tendency_copy)
    trecv[me] = tsend[me]

    def depart_body(j, carry):
        pack(j, lax.rem(me + partner(j), n))
        mig_copy(j).start()
        return carry

    lax.fori_loop(early, n - 1, depart_body, 0)
    pack(n - 1, me)
    own = pltpu.make_async_copy(
        depart.at[pl.ds((n - 1) * mcap, mcap)], arrived_ref.at[pl.ds(me * mcap, mcap)], own_sem)
    own.start()

    def landed_copy(j):
        source = lax.rem(me - partner(j) + n, n)
        return pltpu.make_async_copy(
            landed.at[pl.ds(j * mcap, mcap)], arrived_ref.at[pl.ds(source * mcap, mcap)], l_sem.at[j])

    def landed_body(b, carry):
        note = jnp.zeros((2 * BATCH, width), F32)
        for g in range(per_batch):
            raw_copy(b * per_batch + g).wait_recv()
            note_copy(b * per_batch + g).wait_recv()
            note = note + noted[b * per_batch + g].astype(F32)
        row, lane = iota((BATCH, width), 0), iota((BATCH, width), 1)
        line = jnp.broadcast_to(note[BATCH:BATCH + 1, :], (BATCH, width))
        count = jnp.sum(jnp.where(row == lane, line, 0.0), axis=1, keepdims=True)
        count = jnp.broadcast_to(count, (BATCH, width))
        parts = [slice(g * GROUP, (g + 1) * GROUP) for g in range(BATCH // GROUP)]
        places = [pl.ds(b * BATCH + g * GROUP, GROUP) for g in range(BATCH // GROUP)]
        finals = steps(
            [landed[at].reshape(size, width) for at in places], [note[part] for part in parts],
            [count[part] for part in parts], left, right, across, width)
        for at, final in zip(places, finals):
            landed[at] = final.reshape(GROUP, across, width)
        for g in range(per_batch):
            landed_copy(b * per_batch + g).start()
        return carry

    lax.fori_loop(0, RAW, landed_body, 0)

    crm_copy = pltpu.make_async_copy(crm_ref, crm_hbm, out_sem.at[0])
    crm_copy.start()
    wait_recv(tendency_copy)
    back = lax.dot_general(
        scatter, trecv[...].reshape(table, width), (((0,), (0,)), ((), ())), preferred_element_type=F32)
    new_ref[...] = dyn[...] + back
    new_copy = pltpu.make_async_copy(new_ref, new_hbm, out_sem.at[1])
    new_copy.start()

    wait_send(forcing_copy)
    wait_send(tendency_copy)

    def finish(j, carry):
        mig_copy(j).wait()
        return carry

    lax.fori_loop(raw, n - 1, finish, 0)

    def finish_raw(j, carry):
        raw_copy(j).wait_send()
        note_copy(j).wait_send()
        landed_copy(j).wait()
        return carry

    lax.fori_loop(0, raw, finish_raw, 0)
    own.wait()
    crm_copy.wait()
    new_copy.wait()


def store(*refs):
    count = (len(refs) - 2) // 3
    sources, targets, stages = refs[:count], refs[count:2 * count], refs[2 * count:3 * count]
    sems_in, sems_out = refs[-2:]
    reads, writes = [], []
    for source, target, stage in zip(sources, targets, stages):
        parts = 1 if len(source.shape) == 2 else PIECES
        rows = source.shape[0] // parts
        for i in range(parts):
            at, sem = pl.ds(i * rows, rows), len(reads)
            reads.append(pltpu.make_async_copy(source.at[at], stage.at[at], sems_in.at[sem]))
            writes.append(pltpu.make_async_copy(stage.at[at], target.at[at], sems_out.at[sem]))
    for read in reads:
        read.start()
    for read, write in zip(reads, writes):
        read.wait()
        write.start()
    for write in writes:
        write.wait()


def per_device(gcm_state, cloud_model_state, owner, substeps, neighbours, mig_slot, mig_dest):
    n = lax.axis_size("col")
    cols, width = gcm_state.shape
    slots, across, _ = cloud_model_state.shape
    cap = slots // n
    capp = 16
    while capp <= cap:
        capp *= 2
    listed = mig_slot.shape[0]
    mcap = max(2, 2 * listed // n)
    elements = cols // 9
    hbm = pl.BlockSpec(memory_space=pltpu.HBM)
    anywhere = pl.BlockSpec(memory_space=pl.ANY)
    dma = pltpu.SemaphoreType.DMA
    table = n * capp
    raw = RAW * max(1, BATCH // mcap)
    results = pl.pallas_call(
        functools.partial(kernel, n, cap, capp, mcap),
        out_shape=(
            jax.ShapeDtypeStruct((cols, width), F32),
            jax.ShapeDtypeStruct((slots, across, width), BF16),
            jax.ShapeDtypeStruct((n * mcap, across, width), BF16),
        ),
        in_specs=[hbm] * 7,
        out_specs=(hbm, hbm, hbm),
        scratch_shapes=[
            pltpu.VMEM((cols, width), F32),
            pltpu.VMEM((1, cols), I32),
            pltpu.VMEM((1, cols), I32),
            pltpu.VMEM(neighbours.shape[::-1], I32),
            pltpu.VMEM((1, listed), I32),
            pltpu.VMEM((1, listed), I32),
            pltpu.VMEM((cols, width), F32),
            pltpu.VMEM((slots, across, width), BF16),
            pltpu.VMEM((2 * elements, width), F32),
            pltpu.VMEM((cols, width), F32),
            pltpu.VMEM((n, capp, width), BF16),
            pltpu.VMEM((n, capp, width), BF16),
            pltpu.VMEM((slots + 8, 2 * width), F32),
            pltpu.VMEM((BATCH, 2 * width), F32),
            pltpu.VMEM((slots, width), F32),
            pltpu.VMEM((slots, width), F32),
            pltpu.VMEM((n, capp, width), BF16),
            pltpu.VMEM((n, capp, width), BF16),
            pltpu.VMEM((slots + 1, across, width), BF16),
            pltpu.VMEM((n * mcap, across, width), BF16),
            pltpu.VMEM((raw * mcap, across, width), BF16),
            pltpu.VMEM((raw, 2 * BATCH, width), BF16),
            pltpu.VMEM((raw, 2 * BATCH, width), BF16),
            pltpu.VMEM((1, n * mcap), I32),
            pltpu.SMEM((1, n * mcap), I32),
            dma((2,)), dma((2,)), dma((n,)), dma((n,)), dma((n,)), dma((n,)), dma((n,)), dma((n,)),
            dma, dma((6,)), dma, dma, dma((2,)),
            dma((raw,)), dma((raw,)), dma((raw,)), dma((raw,)), dma((raw,)),
        ],
        compiler_params=pltpu.CompilerParams(
            collective_id=0, has_side_effects=True, vmem_limit_bytes=56 * 1024 * 1024),
        cost_estimate=pl.CostEstimate(flops=5 * 10**9, bytes_accessed=10**7, transcendentals=2 * 10**6),
    )(
        gcm_state, cloud_model_state, owner.reshape(1, cols), substeps.reshape(1, cols),
        neighbours.T, mig_slot.reshape(1, listed), mig_dest.reshape(1, listed),
    )
    return pl.pallas_call(
        store,
        out_shape=tuple(jax.ShapeDtypeStruct(r.shape, r.dtype) for r in results),
        in_specs=[anywhere] * 3, out_specs=(anywhere,) * 3,
        scratch_shapes=[pltpu.VMEM(r.shape, r.dtype) for r in results] + [dma((1 + 2 * PIECES,))] * 2,
        compiler_params=pltpu.CompilerParams(vmem_limit_bytes=56 * 1024 * 1024),
    )(*results)


def solution(mesh):
    wide, deep, flat = P(("ens", "col"), None), P(("ens", "col"), None, None), P(("ens", "col"))
    return jax.shard_map(
        per_device, mesh=mesh,
        in_specs=(wide, deep, wide, flat, wide, flat, wide),
        out_specs=(wide, deep, deep), check_vma=False,
    )
```

```python
import functools

import jax
import jax.numpy as jnp
from jax import lax
from jax.experimental import pallas as pl
from jax.experimental.pallas import tpu as pltpu
from jax.sharding import PartitionSpec as P

F32, BF16, I32 = jnp.float32, jnp.bfloat16, jnp.int32
MESH = pl.DeviceIdType.MESH
GROUP = 8
TOGETHER = 4
BATCH = 16
EARLY = 3
PIECES = 2
RAW = 2


def iota(shape, dim):
    return lax.broadcasted_iota(I32, shape, dim)


def ones_where(condition, dtype=BF16):
    return jnp.where(condition, 1.0, 0.0).astype(dtype)


def exact(a, b):
    return jnp.dot(a, b, preferred_element_type=F32, precision=lax.Precision.HIGHEST)


def fast(a, b):
    return jnp.dot(a, b, preferred_element_type=F32)


def step_matrices(across, width):
    size = GROUP * across
    shift = across.bit_length() - 1
    row, col = iota((size, size), 0), iota((size, size), 1)
    same = (row >> shift) == (col >> shift)
    gap = (row - col) & (across - 1)
    beside = jnp.where((gap == 1) | (gap == across - 1), 1.0, 0.0)
    middle = jnp.where(gap == 0, 3.0, 0.0)
    left = jnp.where(same, beside + middle - 1.5 / across, 0.0).astype(BF16)
    half = width // 2
    source, level = iota((width, 2 * width), 0), iota((width, 2 * width), 1)
    inside = (source < half) == (level < half)
    near = jnp.where(jnp.abs(source - level) == 1, 0.75, 0.0)
    edge = (level == 0) | (level == half - 1) | (level == half) | (level == width - 1)
    near = near - jnp.where(source == level, jnp.where(edge, 0.75, 1.5), 0.0)
    vertical = jnp.where(inside, near, 0.0)
    target = level - width
    sign = jnp.where(target < half, 1.0, -1.0)
    of_level = (source & (half - 1)) == (target & (half - 1))
    phase = jnp.where(of_level, jnp.where(source < half, -0.5, 1.0) * sign, 0.0)
    right = jnp.where(level < width, vertical, phase).astype(BF16)
    rows = iota((GROUP, size), 0)
    total = ones_where(rows == (iota((GROUP, size), 1) >> shift))
    return left, right, total


def steps(states, forcings, counts, left, right, across, width):
    size = GROUP * across
    spread = lambda rows: jnp.broadcast_to(rows[:, None, :], (GROUP, across, width)).reshape(size, width)
    states = list(states)
    for least in (0.5, 1.5):
        linear = [fast(left, state) for state in states]
        levels = [fast(state, right) for state in states]
        moved = [
            0.2 * (a + b[:, :width] + spread(1.5 * f)) + 0.25 * jnp.tanh(b[:, width:])
            for a, b, f in zip(linear, levels, forcings)
        ]
        states = [
            jnp.where(spread(count) > least, new, old.astype(F32)).astype(BF16)
            for new, old, count in zip(moved, states, counts)
        ]
    return states


def kernel(n, cap, capp, mcap,
           gcm_hbm, cloud_hbm, owner_hbm, substeps_hbm, neigh_hbm, slot_hbm, dest_hbm,
           new_hbm, crm_hbm, arrived_ref,
           gcm_ref, owner_ref, substeps_ref, neigh_ref, slot_ref, dest_ref, new_ref, crm_ref, ext, dyn, fsend, frecv, fc, fbatch, keep, tend, tsend, trecv, work, depart,
           landed, notes, noted, pick_v, pick,
           halo_send, halo_recv, f_send, f_recv, t_send, t_recv, m_send, m_recv, own_sem,
           in_sem, cloud_sem, pick_sem, out_sem,
           r_send, r_recv, g_send, g_recv, l_sem):
    me = lax.axis_index("col")
    cols, width = gcm_hbm.shape
    slots, across, _ = cloud_hbm.shape
    listed = slot_hbm.shape[1]
    elements = cols // 9
    margin = elements // 2
    table = n * capp
    spots = n * mcap
    shift = capp.bit_length() - 1
    right_dev, left_dev = lax.rem(me + 1, n), lax.rem(me + n - 1, n)

    barrier = pltpu.get_barrier_semaphore()

    def greet(k, carry):
        pl.semaphore_signal(barrier, inc=1, device_id={"col": lax.rem(me + k, n)}, device_id_type=MESH)
        return carry

    lax.fori_loop(1, n, greet, 0)

    inputs = [
        pltpu.make_async_copy(source, target, in_sem.at[i])
        for i, (source, target) in enumerate([
            (gcm_hbm, gcm_ref), (owner_hbm, owner_ref), (substeps_hbm, substeps_ref),
            (neigh_hbm, neigh_ref), (slot_hbm, slot_ref), (dest_hbm, dest_ref)])
    ]
    for copy in inputs:
        copy.start()
    cloud_copy = pltpu.make_async_copy(cloud_hbm, work.at[pl.ds(0, slots)], cloud_sem)
    cloud_copy.start()
    for copy in inputs:
        copy.wait()
    gcm = gcm_ref[...]
    place = iota((elements, cols), 1) - 9 * iota((elements, cols), 0)
    member = ones_where((place >= 0) & (place < 9), F32)
    means = exact(member, gcm) * (1.0 / 9.0)
    ext[pl.ds(margin, elements), :] = means
    slot_row, dest_row = slot_ref[...], dest_ref[...]
    slot_col = jnp.broadcast_to(slot_row, (listed, listed)).T
    dest_col = jnp.broadcast_to(dest_row, (listed, listed)).T
    same = (dest_col == dest_row) & (iota((listed, listed), 1) < iota((listed, listed), 0))
    place_mig = dest_col[:, 0:1] * mcap + jnp.sum(jnp.where(same, 1, 0), axis=1, keepdims=True)
    found = iota((listed, spots), 1) == place_mig
    chosen = jnp.sum(jnp.where(found, slot_col[:, 0:1] - slots, 0), axis=0, keepdims=True) + slots
    pick_v[...] = chosen
    pick_copy = pltpu.make_async_copy(pick_v, pick, pick_sem)
    pick_copy.start()
    work[pl.ds(slots, 1)] = jnp.zeros((1, across, width), BF16)
    pick_copy.wait()
    pl.semaphore_wait(barrier, n - 1)

    up = pltpu.make_async_remote_copy(
        src_ref=ext.at[pl.ds(elements, margin)], dst_ref=ext.at[pl.ds(0, margin)],
        send_sem=halo_send.at[0], recv_sem=halo_recv.at[0],
        device_id={"col": right_dev}, device_id_type=MESH)
    down = pltpu.make_async_remote_copy(
        src_ref=ext.at[pl.ds(margin, margin)], dst_ref=ext.at[pl.ds(margin + elements, margin)],
        send_sem=halo_send.at[1], recv_sem=halo_recv.at[1],
        device_id={"col": left_dev}, device_id_type=MESH)
    up.start()
    down.start()

    def partner(j):
        half = lax.div(j + 1, 2)
        return n // 2 + jnp.where(lax.rem(j, 2) == 1, -half, half)

    def mig_copy(j):
        k = partner(j)
        return pltpu.make_async_remote_copy(
            src_ref=depart.at[pl.ds(j * mcap, mcap)],
            dst_ref=arrived_ref.at[pl.ds(me * mcap, mcap)],
            send_sem=m_send.at[k], recv_sem=m_recv.at[k],
            device_id={"col": lax.rem(me + k, n)}, device_id_type=MESH)

    per_batch = max(1, BATCH // mcap)
    raw = RAW * per_batch

    def raw_copy(j):
        return pltpu.make_async_remote_copy(
            src_ref=depart.at[pl.ds(j * mcap, mcap)], dst_ref=landed.at[pl.ds(j * mcap, mcap)],
            send_sem=r_send.at[j], recv_sem=r_recv.at[j],
            device_id={"col": lax.rem(me + partner(j), n)}, device_id_type=MESH)

    def pack(j, dest):
        for r in range(mcap):
            depart[j * mcap + r] = work[pick[0, dest * mcap + r]]

    def raw_body(j, carry):
        pack(j, lax.rem(me + partner(j), n))
        raw_copy(j).start()
        return carry

    cloud_copy.wait()
    lax.fori_loop(0, raw // 2, raw_body, 0)

    owner_row = owner_ref[...]
    hits = iota((n, cols), 0) == owner_row
    earlier = ones_where(iota((cols, cols), 0) < iota((cols, cols), 1))
    before = fast(ones_where(hits), earlier)
    rank = jnp.sum(jnp.where(hits, before, 0.0), axis=0, keepdims=True).astype(I32)
    place_row = owner_row * capp + rank
    scatter = ones_where(iota((table, cols), 0) == place_row)
    p_col = iota((table, cols), 0)
    count_row = ones_where(((p_col & (capp - 1)) == cap) & ((p_col >> shift) == owner_row))
    count_lane = jnp.where(iota((width, cols), 0) == rank, substeps_ref[...].astype(F32), 0.0).astype(BF16)
    sent_counts = lax.dot_general(count_row, count_lane, (((1,), (1,)), ((), ())), preferred_element_type=F32)
    fsend[...] = sent_counts.astype(BF16).reshape(n, capp, width)

    ids = neigh_ref[...] - me * elements + margin
    span = elements * n
    ids = jnp.where(ids < 0, ids + span, ids)
    ids = jnp.where(ids >= span, ids - span, ids)
    tall = iota((elements + 2 * margin, elements), 0)
    weights = jnp.where(tall == iota((elements + 2 * margin, elements), 1) + margin, -4.0, 0.0)
    for k in range(neigh_ref.shape[0]):
        weights = weights + jnp.where(tall == ids[k:k + 1, :], 1.0, 0.0)
    spread_gap = iota((cols, elements), 0) - 9 * iota((cols, elements), 1)
    spread = ones_where((spread_gap >= 0) & (spread_gap < 9), F32)
    per_column = fast(spread.astype(BF16), weights.T.astype(BF16))

    up.wait()
    down.wait()
    state = gcm + 0.2 * exact(per_column, ext[...])
    dyn[...] = state
    sent = fast(scatter, state.astype(BF16)) + fsend[...].reshape(table, width).astype(F32)
    fsend[...] = sent.astype(BF16).reshape(n, capp, width)

    def forcing_copy(k):
        return pltpu.make_async_remote_copy(
            src_ref=fsend.at[lax.rem(me + k, n)], dst_ref=frecv.at[me],
            send_sem=f_send.at[k], recv_sem=f_recv.at[k],
            device_id={"col": lax.rem(me + k, n)}, device_id_type=MESH)

    def start(copy):
        def body(k, carry):
            copy(k).start()
            return carry
        lax.fori_loop(1, n, body, 0)

    def wait_recv(copy):
        def body(k, carry):
            copy(k).wait_recv()
            return carry
        lax.fori_loop(1, n, body, 0)

    def wait_send(copy):
        def body(k, carry):
            copy(k).wait_send()
            return carry
        lax.fori_loop(1, n, body, 0)

    start(forcing_copy)
    lax.fori_loop(raw // 2, raw, raw_body, 0)
    frecv[me] = fsend[me]

    gone = iota((slots, listed), 0) == slot_ref[...]
    gone = jnp.max(jnp.where(gone, 1.0, 0.0), axis=1, keepdims=True)
    keep[...] = jnp.broadcast_to(1.0 - gone, (slots, width))
    fc[pl.ds(slots, 8), :] = jnp.zeros((8, 2 * width), F32)
    left, right, total = step_matrices(across, width)
    p_lane = iota((slots, table), 1)
    q_lane = (p_lane >> shift) * cap + (p_lane & (capp - 1))
    compact = ones_where((q_lane == iota((slots, table), 0)) & ((p_lane & (capp - 1)) < cap))
    first = (p_lane >> shift) * cap
    q_table = iota((slots, table), 0)
    counting = ones_where(((p_lane & (capp - 1)) == cap) & (q_table >= first) & (q_table < first + cap))
    within = fast(compact, ones_where((iota((table, width), 0) & (capp - 1)) == iota((table, width), 1)))

    wait_recv(forcing_copy)
    received = frecv[...].reshape(table, width)
    fc[pl.ds(0, slots), 0:width] = fast(compact, received)
    count = jnp.sum(fast(counting, received) * within, axis=1, keepdims=True)
    fc[pl.ds(0, slots), width:2 * width] = jnp.broadcast_to(count, (slots, width))

    early = (RAW + EARLY) * per_batch
    size = GROUP * across

    def note_copy(j):
        return pltpu.make_async_remote_copy(
            src_ref=notes.at[j], dst_ref=noted.at[j],
            send_sem=g_send.at[j], recv_sem=g_recv.at[j],
            device_id={"col": lax.rem(me + partner(j), n)}, device_id_type=MESH)

    def note_body(b, carry):
        for i in range(BATCH):
            j = b * per_batch + i // mcap
            at = pick[0, lax.rem(me + partner(j), n) * mcap + i % mcap]
            fbatch[i:i + 1, :] = fc[pl.ds(at, 1), :]
        forcing, count = fbatch[:, 0:width], fbatch[:, width:2 * width]
        row, lane = iota((BATCH, width), 0), iota((BATCH, width), 1)
        for g in range(per_batch):
            mine = (row >= g * mcap) & (row < (g + 1) * mcap)
            line = jnp.sum(jnp.where(mine & (row == lane), count, 0.0), axis=0, keepdims=True)
            lower = jnp.where(row == 0, jnp.broadcast_to(line, (BATCH, width)), 0.0)
            notes[b * per_batch + g] = jnp.concatenate(
                [jnp.where(mine, forcing, 0.0), lower], axis=0).astype(BF16)
            note_copy(b * per_batch + g).start()
        return carry

    lax.fori_loop(0, RAW, note_body, 0)

    def early_body(b, carry):
        for i in range(BATCH):
            j = b * per_batch + i // mcap
            at = pick[0, lax.rem(me + partner(j), n) * mcap + i % mcap]
            depart[b * BATCH + i] = work[at]
            fbatch[i:i + 1, :] = fc[pl.ds(at, 1), :]
        forcings, counts, states = [], [], []
        for g in range(BATCH // GROUP):
            states.append(depart[pl.ds(b * BATCH + g * GROUP, GROUP)].reshape(size, width))
            forcings.append(fbatch[g * GROUP:(g + 1) * GROUP, 0:width])
            counts.append(fbatch[g * GROUP:(g + 1) * GROUP, width:2 * width])
        finals = steps(states, forcings, counts, left, right, across, width)
        for g, final in enumerate(finals):
            depart[pl.ds(b * BATCH + g * GROUP, GROUP)] = final.reshape(GROUP, across, width)
        for j in range(per_batch):
            mig_copy(b * per_batch + j).start()
        return carry

    lax.fori_loop(RAW, RAW + EARLY, early_body, 0)

    def chunk(c, carry):
        rows = [pl.ds(pl.multiple_of((c * TOGETHER + g) * GROUP, GROUP), GROUP) for g in range(TOGETHER)]
        forcings = [fc[row, 0:width] for row in rows]
        counts = [fc[row, width:2 * width] for row in rows]
        stays = [keep[row, :] for row in rows]
        begins = [work[row].reshape(size, width) for row in rows]
        finals = steps(begins, forcings, counts, left, right, across, width)
        gains = [fast(total, final) - fast(total, begin) for final, begin in zip(finals, begins)]
        for row, final, gain, count, stay in zip(rows, finals, gains, counts, stays):
            tend[row, :] = gain * (1.0 / across) / jnp.maximum(count, 1.0)
            work[row] = final.reshape(GROUP, across, width)
            stay = jnp.broadcast_to(stay[:, None, :], (GROUP, across, width)).astype(BF16)
            crm_ref[row] = final.reshape(GROUP, across, width) * stay
        return carry

    lax.fori_loop(0, slots // (GROUP * TOGETHER), chunk, 0)

    p_row = iota((table, slots), 0)
    q_row = (p_row >> shift) * cap + (p_row & (capp - 1))
    expand = ones_where((q_row == iota((table, slots), 1)) & ((p_row & (capp - 1)) < cap))
    tsend[...] = fast(expand, tend[...].astype(BF16)).astype(BF16).reshape(n, capp, width)

    def tendency_copy(k):
        return pltpu.make_async_remote_copy(
            src_ref=tsend.at[lax.rem(me + k, n)], dst_ref=trecv.at[me],
            send_sem=t_send.at[k], recv_sem=t_recv.at[k],
            device_id={"col": lax.rem(me + k, n)}, device_id_type=MESH)

    start(tendency_copy)
    trecv[me] = tsend[me]

    def depart_body(j, carry):
        pack(j, lax.rem(me + partner(j), n))
        mig_copy(j).start()
        return carry

    lax.fori_loop(early, n - 1, depart_body, 0)
    pack(n - 1, me)
    own = pltpu.make_async_copy(
        depart.at[pl.ds((n - 1) * mcap, mcap)], arrived_ref.at[pl.ds(me * mcap, mcap)], own_sem)
    own.start()

    def landed_copy(j):
        source = lax.rem(me - partner(j) + n, n)
        return pltpu.make_async_copy(
            landed.at[pl.ds(j * mcap, mcap)], arrived_ref.at[pl.ds(source * mcap, mcap)], l_sem.at[j])

    def landed_body(b, carry):
        note = jnp.zeros((2 * BATCH, width), F32)
        for g in range(per_batch):
            raw_copy(b * per_batch + g).wait_recv()
            note_copy(b * per_batch + g).wait_recv()
            note = note + noted[b * per_batch + g].astype(F32)
        row, lane = iota((BATCH, width), 0), iota((BATCH, width), 1)
        line = jnp.broadcast_to(note[BATCH:BATCH + 1, :], (BATCH, width))
        count = jnp.sum(jnp.where(row == lane, line, 0.0), axis=1, keepdims=True)
        count = jnp.broadcast_to(count, (BATCH, width))
        parts = [slice(g * GROUP, (g + 1) * GROUP) for g in range(BATCH // GROUP)]
        places = [pl.ds(b * BATCH + g * GROUP, GROUP) for g in range(BATCH // GROUP)]
        finals = steps(
            [landed[at].reshape(size, width) for at in places], [note[part] for part in parts],
            [count[part] for part in parts], left, right, across, width)
        for at, final in zip(places, finals):
            landed[at] = final.reshape(GROUP, across, width)
        for g in range(per_batch):
            landed_copy(b * per_batch + g).start()
        return carry

    lax.fori_loop(0, RAW, landed_body, 0)

    crm_copy = pltpu.make_async_copy(crm_ref, crm_hbm, out_sem.at[0])
    crm_copy.start()
    wait_recv(tendency_copy)
    back = lax.dot_general(
        scatter, trecv[...].reshape(table, width), (((0,), (0,)), ((), ())), preferred_element_type=F32)
    new_ref[...] = dyn[...] + back
    new_copy = pltpu.make_async_copy(new_ref, new_hbm, out_sem.at[1])
    new_copy.start()

    wait_send(forcing_copy)
    wait_send(tendency_copy)

    def finish(j, carry):
        mig_copy(j).wait()
        return carry

    lax.fori_loop(raw, n - 1, finish, 0)

    def finish_raw(j, carry):
        raw_copy(j).wait_send()
        note_copy(j).wait_send()
        landed_copy(j).wait()
        return carry

    lax.fori_loop(0, raw, finish_raw, 0)
    own.wait()
    crm_copy.wait()
    new_copy.wait()


def store(*refs):
    count = (len(refs) - 2) // 3
    sources, targets, stages = refs[:count], refs[count:2 * count], refs[2 * count:3 * count]
    sems_in, sems_out = refs[-2:]
    reads, writes = [], []
    for source, target, stage in zip(sources, targets, stages):
        parts = 1 if len(source.shape) == 2 else PIECES
        rows = source.shape[0] // parts
        for i in range(parts):
            at, sem = pl.ds(i * rows, rows), len(reads)
            reads.append(pltpu.make_async_copy(source.at[at], stage.at[at], sems_in.at[sem]))
            writes.append(pltpu.make_async_copy(stage.at[at], target.at[at], sems_out.at[sem]))
    for read in reads:
        read.start()
    for read, write in zip(reads, writes):
        read.wait()
        write.start()
    for write in writes:
        write.wait()


def per_device(gcm_state, cloud_model_state, owner, substeps, neighbours, mig_slot, mig_dest):
    n = lax.axis_size("col")
    cols, width = gcm_state.shape
    slots, across, _ = cloud_model_state.shape
    cap = slots // n
    capp = 16
    while capp <= cap:
        capp *= 2
    listed = mig_slot.shape[0]
    mcap = max(2, 2 * listed // n)
    elements = cols // 9
    hbm = pl.BlockSpec(memory_space=pltpu.HBM)
    anywhere = pl.BlockSpec(memory_space=pl.ANY)
    dma = pltpu.SemaphoreType.DMA
    table = n * capp
    raw = RAW * max(1, BATCH // mcap)
    results = pl.pallas_call(
        functools.partial(kernel, n, cap, capp, mcap),
        out_shape=(
            jax.ShapeDtypeStruct((cols, width), F32),
            jax.ShapeDtypeStruct((slots, across, width), BF16),
            jax.ShapeDtypeStruct((n * mcap, across, width), BF16),
        ),
        in_specs=[hbm] * 7,
        out_specs=(hbm, hbm, hbm),
        scratch_shapes=[
            pltpu.VMEM((cols, width), F32),
            pltpu.VMEM((1, cols), I32),
            pltpu.VMEM((1, cols), I32),
            pltpu.VMEM(neighbours.shape[::-1], I32),
            pltpu.VMEM((1, listed), I32),
            pltpu.VMEM((1, listed), I32),
            pltpu.VMEM((cols, width), F32),
            pltpu.VMEM((slots, across, width), BF16),
            pltpu.VMEM((2 * elements, width), F32),
            pltpu.VMEM((cols, width), F32),
            pltpu.VMEM((n, capp, width), BF16),
            pltpu.VMEM((n, capp, width), BF16),
            pltpu.VMEM((slots + 8, 2 * width), F32),
            pltpu.VMEM((BATCH, 2 * width), F32),
            pltpu.VMEM((slots, width), F32),
            pltpu.VMEM((slots, width), F32),
            pltpu.VMEM((n, capp, width), BF16),
            pltpu.VMEM((n, capp, width), BF16),
            pltpu.VMEM((slots + 1, across, width), BF16),
            pltpu.VMEM((n * mcap, across, width), BF16),
            pltpu.VMEM((raw * mcap, across, width), BF16),
            pltpu.VMEM((raw, 2 * BATCH, width), BF16),
            pltpu.VMEM((raw, 2 * BATCH, width), BF16),
            pltpu.VMEM((1, n * mcap), I32),
            pltpu.SMEM((1, n * mcap), I32),
            dma((2,)), dma((2,)), dma((n,)), dma((n,)), dma((n,)), dma((n,)), dma((n,)), dma((n,)),
            dma, dma((6,)), dma, dma, dma((2,)),
            dma((raw,)), dma((raw,)), dma((raw,)), dma((raw,)), dma((raw,)),
        ],
        compiler_params=pltpu.CompilerParams(
            collective_id=0, has_side_effects=True, vmem_limit_bytes=56 * 1024 * 1024),
        cost_estimate=pl.CostEstimate(flops=5 * 10**9, bytes_accessed=10**7, transcendentals=2 * 10**6),
    )(
        gcm_state, cloud_model_state, owner.reshape(1, cols), substeps.reshape(1, cols),
        neighbours.T, mig_slot.reshape(1, listed), mig_dest.reshape(1, listed),
    )
    return pl.pallas_call(
        store,
        out_shape=tuple(jax.ShapeDtypeStruct(r.shape, r.dtype) for r in results),
        in_specs=[anywhere] * 3, out_specs=(anywhere,) * 3,
        scratch_shapes=[pltpu.VMEM(r.shape, r.dtype) for r in results] + [dma((1 + 2 * PIECES,))] * 2,
        compiler_params=pltpu.CompilerParams(vmem_limit_bytes=56 * 1024 * 1024),
    )(*results)


def solution(mesh):
    wide, deep, flat = P(("ens", "col"), None), P(("ens", "col"), None, None), P(("ens", "col"))
    return jax.shard_map(
        per_device, mesh=mesh,
        in_specs=(wide, deep, wide, flat, wide, flat, wide),
        out_specs=(wide, deep, deep), check_vma=False,
    )
```
